256 devices in a mesh: dp: 4 (over y_lo, core), expert: 8 (over z), tensor: 8 (over x, y_hi).
Axes of the slice: x: 4, y: 4 (y_hi: 2, y_lo: 2; y = y_hi * 2 + y_lo), z: 8, core: 2. Of those that a mesh axis runs over, the one named last changes fastest.
Arguments:
- grad_out: bfloat16 [32768, 2048], P(('dp', 'expert', 'tensor')), may hold values from -6 to 6
- expert_ids: int32 [32768, 2], P(('dp', 'expert', 'tensor')), may hold values from 0 to 63, all different within a row; in each aligned block of 128 rows (0 to 127, 128 to 255, ...) at most 5 rows name the same one
- gate_weights: float32 [32768, 2], P(('dp', 'expert', 'tensor')), may hold values from 0.05 to 0.6
- overflow: int32 [32768, 2], P(('dp', 'expert', 'tensor')), may hold values 0 or 1
- saved_gate: bfloat16 [64, 4, 64, 5, 1408], P(('expert', 'tensor'), None, None, None, 'dp'), may hold values from -6 to 6
- saved_up: bfloat16 [64, 4, 64, 5, 1408], P(('expert', 'tensor'), None, None, None, 'dp'), may hold values from -6 to 6
- w_gate: bfloat16 [64, 2048, 1408], P(('expert', 'tensor'), None, 'dp'), may hold values from -0.125 to 0.125
- w_up: bfloat16 [64, 2048, 1408], P(('expert', 'tensor'), None, 'dp'), may hold values from -0.125 to 0.125
- w_down: bfloat16 [64, 1408, 2048], P(('expert', 'tensor'), 'dp'), may hold values from -0.15625 to 0.15625
- shared_gate_act: bfloat16 [32768, 1408], P(('dp', 'expert'), 'tensor'), may hold values from -6 to 6
- shared_up_act: bfloat16 [32768, 1408], P(('dp', 'expert'), 'tensor'), may hold values from -6 to 6
- ws_gate: bfloat16 [2048, 1408], P(None, 'tensor'), may hold values from -0.125 to 0.125
- ws_up: bfloat16 [2048, 1408], P(None, 'tensor'), may hold values from -0.125 to 0.125
- ws_down: bfloat16 [1408, 2048], P('tensor'), may hold values from -0.15625 to 0.15625
- w_out: bfloat16 [2048, 2048], P('tensor'), may hold values from -0.125 to 0.125
Outputs:
- grad_hidden: bfloat16 [32768, 2048], P(('dp', 'expert', 'tensor'))
- grad_context: bfloat16 [32768, 2048], P(('dp', 'expert'), 'tensor')
The draws below stay inside these ranges and needn't reach their ends.
Inputs may be any that keep to these rules, and one draw needn't show every extreme that they name: `expert_ids`: each row names 2 different experts; within the rows of one device (aligned blocks of 128 rows) no expert is named by more than 5 rows, a bound that some block reaches.
All inputs are finite; a program needn't handle non-finite values. No bound on the sum of `overflow` on one device may be relied on, other than what follows from the above.
Results may differ from the reference program's by a relative error of at most 0.015.
Values may be sent and summed in bfloat16 or wider, within the bound.
A program may use at most 128 MiB of HBM per device.

```python
import math
import jax
import jax.numpy as jnp
import numpy as np
from jax import lax

D = 2048
FE = 1408
FS = 1408
EXPERTS = 64
TOPK = 2
HV = 2048
TOK_DEV = 128
CAP = 5
TOKENS = 32768
N_DP = 4
N_EXPERT = 8
N_TENSOR = 8
DEVICES = 256


def with_ends(array, stream_key, least, high):
    extent = array.shape
    place = [jax.random.randint(jax.random.fold_in(stream_key, axis), (), 0, extent[axis]) for axis in range(len(extent))]
    array = array.at[tuple(place)].set(least)
    longest = extent.index(max(extent))
    place[longest] = (place[longest] + 1) % extent[longest]
    return array.at[tuple(place)].set(high)


def level_of(rng, dims, split, smallest, largest):
    def one(axis_at, parts):
        heights = jax.random.uniform(jax.random.fold_in(jax.random.fold_in(rng, 6), axis_at), (parts,), jnp.float32, smallest / len(split), largest / len(split))
        return jnp.repeat(jnp.exp(heights), dims[axis_at] // parts).reshape((-1,) + (1,) * (len(dims) - axis_at - 1))

    level = one(*split[0])
    for cut in split[1:]:
        level = level * one(*cut)
    return level


def assign_block(own_key, own, number, rows, amount, top, bound, lean):
    ranking = jax.random.permutation(own_key, amount)
    heavy_load, ordinary = shares(amount, rows * top, bound, lean, True), shares(amount, rows * top, bound, lean, False)
    places = jnp.arange(amount)

    def named(tallies, rotation):
        used = int((tallies > 0).sum())
        fixed = max(1, used // 4)
        shifted = fixed + (places - fixed + rotation * (used - fixed)) % max(1, amount - fixed)
        return jnp.zeros((amount,), jnp.int32).at[ranking[jnp.where(places < fixed, places, shifted)]].set(jnp.asarray(tallies, jnp.int32))

    tallies = jnp.where(number % 4 == 0, named(heavy_load, number // 4), named(ordinary, number - number // 4 - 1))
    mixed = jax.random.permutation(jax.random.fold_in(own, 3), amount)
    giver, receiver = mixed[0:amount // 2 * 2:2], mixed[1:amount // 2 * 2:2]
    room = jnp.minimum(tallies[giver] - 1, bound - tallies[receiver]) // 2
    room = jnp.where((giver == ranking[0]) | (receiver == ranking[0]) | (tallies[receiver] == 0), 0, jnp.maximum(room, 0))
    shifted = jax.random.randint(jax.random.fold_in(own, 4), (amount // 2,), 0, 1 << 20) % (room + 1)
    tallies = tallies.at[giver].add(-shifted).at[receiver].add(shifted)
    items = jnp.searchsorted(jnp.cumsum(tallies), jnp.arange(rows * top), side="right").astype(jnp.int32)
    table = items.reshape(top, rows).T
    table = table[jax.random.permutation(jax.random.fold_in(own, 1), rows)]
    rotation = jax.random.randint(jax.random.fold_in(own, 2), (rows, 1), 0, top)
    return jnp.take_along_axis(table, (jnp.arange(top)[None, :] + rotation) % top, axis=1)


def shares(count, total, limit, slope, full):
    weights = [(1 << 20) // math.isqrt(standing ** slope) + 1 for standing in range(1, count + 1)]
    largest = limit if full else min(limit, max(-(-total // count), total * weights[0] // sum(weights)))
    least = 1 if total - largest >= count - 1 else 0
    holding, spare = [largest] + [least] * (count - 1), total - largest - least * (count - 1)
    while spare > 0:
        candidates = [i for i in range(1, count) if holding[i] < largest] or [i for i in range(1, count) if holding[i] < limit]
        pool, left = sum([weights[i] for i in candidates]), spare
        for i in candidates:
            addition = min(limit - holding[i], max(1, left * weights[i] // pool), spare)
            holding[i] = holding[i] + addition
            spare = spare - addition
    return np.array(holding)


def normal_values(key, extent, deviation, bound, cuts=(), kind=jnp.bfloat16):
    entries = jax.random.normal(key, extent, jnp.float32) * deviation
    if len(cuts) > 0:
        entries = level_of(key, extent, cuts, -0.22, 0.18) * entries
    return jnp.clip(entries, min=-bound, max=bound).astype(kind)


def setup_inputs(seed: int = 0) -> dict:
    key_list = jax.random.split(jax.random.key(seed), 16)
    grad_out = normal_values(key_list[0], (TOKENS, D), 1.0, 6.0, ((0, 256),))
    expert_ids_keys = jax.random.split(jax.random.fold_in(key_list[1], 1), TOKENS // TOK_DEV)
    expert_ids_turns = jax.random.permutation(jax.random.fold_in(key_list[1], 3), TOKENS // TOK_DEV)
    expert_ids = jax.vmap(lambda own, number: assign_block(jax.random.fold_in(key_list[1], 2), own, number, TOK_DEV, EXPERTS, TOPK, CAP, 2))(expert_ids_keys, expert_ids_turns).reshape((TOKENS, TOPK))
    gate_weights = jnp.clip(jnp.exp(math.log(0.6) - 2.4849067 * jax.random.uniform(key_list[2], (TOKENS, TOPK), jnp.float32) ** level_of(key_list[2], (TOKENS, TOPK), ((0, 256),), -0.2, 0.2)), 0.05, 0.6)
    overflow = with_ends((jax.random.randint(key_list[3], (TOKENS, TOPK), 0, 4) < 1).astype(jnp.int32), jax.random.fold_in(key_list[3], 1), 0, 1)
    saved_gate = normal_values(key_list[4], (EXPERTS, N_DP, N_EXPERT * N_TENSOR, CAP, FE), 1.0, 6.0, ((0, 64), (4, 4)))
    saved_up = normal_values(key_list[5], (EXPERTS, N_DP, N_EXPERT * N_TENSOR, CAP, FE), 1.0, 6.0, ((0, 64), (4, 4)))
    w_gate = normal_values(key_list[6], (EXPERTS, D, FE), D ** -0.5, 0.125, ((0, 64), (2, 4)))
    w_up = normal_values(key_list[7], (EXPERTS, D, FE), D ** -0.5, 0.125, ((0, 64), (2, 4)))
    w_down = normal_values(key_list[8], (EXPERTS, FE, D), FE ** -0.5, 0.15625, ((0, 64), (1, 4)))
    shared_gate_act = normal_values(key_list[9], (TOKENS, FS), 1.0, 6.0, ((0, 32), (1, 8)))
    shared_up_act = normal_values(key_list[10], (TOKENS, FS), 1.0, 6.0, ((0, 32), (1, 8)))
    ws_gate = normal_values(key_list[11], (D, FS), D ** -0.5, 0.125, ((1, 8),))
    ws_up = normal_values(key_list[12], (D, FS), D ** -0.5, 0.125, ((1, 8),))
    ws_down = normal_values(key_list[13], (FS, D), FS ** -0.5, 0.15625, ((0, 8),))
    w_out = normal_values(key_list[14], (HV, D), HV ** -0.5, 0.125, ((0, 8),))
    return dict(grad_out=grad_out, expert_ids=expert_ids, gate_weights=gate_weights, overflow=overflow, saved_gate=saved_gate, saved_up=saved_up, w_gate=w_gate, w_up=w_up, w_down=w_down, shared_gate_act=shared_gate_act, shared_up_act=shared_up_act, ws_gate=ws_gate, ws_up=ws_up, ws_down=ws_down, w_out=w_out)


def swiglu_backward(hidden_activation, gate_act, up_act):
    gate_value = gate_act.astype(jnp.float32)
    sigmoid_value = jax.nn.sigmoid(gate_value)
    gate_input_gradient = (hidden_activation * up_act.astype(jnp.float32) * sigmoid_value * (1.0 + gate_value * (1.0 - sigmoid_value))).astype(jnp.bfloat16)
    up_input_gradient = (hidden_activation * gate_value * sigmoid_value).astype(jnp.bfloat16)
    return gate_input_gradient, up_input_gradient


def reference(grad_out, expert_ids, gate_weights, overflow, saved_gate, saved_up, w_gate, w_up, w_down, shared_gate_act, shared_up_act, ws_gate, ws_up, ws_down, w_out):
    flag_values = overflow.astype(jnp.float32)
    routed_weight = (gate_weights * (1.0 - flag_values)).astype(jnp.bfloat16)
    shared_weight = 1.0 + jnp.sum(gate_weights * flag_values, axis=1)
    routed_grad = (grad_out.astype(jnp.float32)[:, None, :] * routed_weight.astype(jnp.float32)[:, :, None]).astype(jnp.bfloat16)
    pair_block = TOK_DEV * TOPK
    block_ids = expert_ids.reshape(DEVICES, pair_block)
    onehot = (block_ids[:, :, None] == jnp.arange(EXPERTS, dtype=jnp.int32)[None, None, :]).astype(jnp.int32)
    earlier = jnp.cumsum(onehot, axis=1) - onehot
    slot = jnp.sum(earlier * onehot, axis=2)
    block_index = jnp.arange(DEVICES, dtype=jnp.int32)[:, None]
    slot_place = (block_ids * DEVICES + block_index) * CAP + slot
    pair_index = jnp.arange(TOKENS * TOPK, dtype=jnp.int32).reshape(DEVICES, pair_block)
    slot_owner = jnp.full((EXPERTS * DEVICES * CAP,), TOKENS * TOPK, jnp.int32)
    slot_owner = slot_owner.at[slot_place.reshape(-1)].set(pair_index.reshape(-1)).reshape(EXPERTS, DEVICES * CAP)
    rows_all = jnp.concatenate([routed_grad.reshape(TOKENS * TOPK, D), jnp.zeros((1, D), jnp.bfloat16)], axis=0)
    group_width = FE // N_DP

    def one_expert(totals, expert_index):
        picked = slot_owner[expert_index]
        capacity_slot_rows = rows_all[picked]
        gate_act = saved_gate[expert_index].reshape(DEVICES * CAP, FE)
        up_act = saved_up[expert_index].reshape(DEVICES * CAP, FE)
        hidden_activation = jnp.dot(capacity_slot_rows, w_down[expert_index].T, preferred_element_type=jnp.float32)
        gate_input_gradient, up_input_gradient = swiglu_backward(hidden_activation, gate_act, up_act)
        gate_projection_weight = w_gate[expert_index]
        up_projection_weight = w_up[expert_index]
        expert_term = jnp.zeros((DEVICES * CAP, D), jnp.float32)
        for group_index in range(N_DP):
            low = group_index * group_width
            high = low + group_width
            quarter_term = jnp.dot(gate_input_gradient[:, low:high], gate_projection_weight[:, low:high].T, preferred_element_type=jnp.float32)
            quarter_term = quarter_term + jnp.dot(up_input_gradient[:, low:high], up_projection_weight[:, low:high].T, preferred_element_type=jnp.float32)
            quarter_term = lax.optimization_barrier(quarter_term.astype(jnp.bfloat16))
            expert_term = expert_term + quarter_term.astype(jnp.float32)
        token_row = picked // TOPK
        return totals.at[token_row].add(expert_term), None

    totals, unused = lax.scan(one_expert, jnp.zeros((TOKENS + 1, D), jnp.float32), jnp.arange(EXPERTS, dtype=jnp.int32))
    routed_total = totals[:TOKENS].astype(jnp.bfloat16)

    shared_grad = (grad_out.astype(jnp.float32) * shared_weight[:, None]).astype(jnp.bfloat16)
    shared_hidden = jnp.dot(shared_grad, ws_down.T, preferred_element_type=jnp.float32)
    shared_gate_grad, shared_up_grad = swiglu_backward(shared_hidden, shared_gate_act, shared_up_act)
    part_width = FS // N_TENSOR
    shared_total = jnp.zeros((TOKENS, D), jnp.float32)
    for group_index in range(N_TENSOR):
        low = group_index * part_width
        high = low + part_width
        group_term = jnp.dot(shared_gate_grad[:, low:high], ws_gate[:, low:high].T, preferred_element_type=jnp.float32)
        group_term = group_term + jnp.dot(shared_up_grad[:, low:high], ws_up[:, low:high].T, preferred_element_type=jnp.float32)
        group_term = lax.optimization_barrier(group_term.astype(jnp.bfloat16))
        shared_total = shared_total + group_term.astype(jnp.float32)
    grad_hidden = (grad_out.astype(jnp.float32) + shared_total + routed_total.astype(jnp.float32)).astype(jnp.bfloat16)
    grad_context = jnp.dot(grad_hidden, w_out.T, preferred_element_type=jnp.float32).astype(jnp.bfloat16)
    return grad_hidden, grad_context
```

```python
import functools

import jax
import jax.numpy as jnp
from jax import lax
from jax.experimental import pallas as pl
from jax.experimental.pallas import tpu as pltpu
from jax.sharding import PartitionSpec as P

MESH = pl.DeviceIdType.MESH
BF = jnp.bfloat16
F32 = jnp.float32
CHUNKS = 2
TOK = 128
D = 2048
WIDTH = D // CHUNKS
CAP = 5
PLANE = CAP * 8
ROWS = 8 * PLANE
FE = 352
FS = 176
DEPTH = 768
N_SEM = 160


def nn(a, b):
    return jnp.dot(a, b, preferred_element_type=F32)


def nt(a, b):
    return lax.dot_general(a, b, (((1,), (1,)), ((), ())), preferred_element_type=F32)


def swiglu_backward(hidden, gate_act, up_act):
    s = jax.nn.sigmoid(gate_act)
    gate = hidden * up_act * s * (1.0 + gate_act * (1.0 - s))
    up = hidden * gate_act * s
    return gate, up


def rows_of(planes):
    return planes.astype(F32).reshape(ROWS, planes.shape[-1])


def kernel(
    grad_ref, ids_ref, gw_ref, ov_ref, sgate_hbm, sup_hbm, wg_hbm, wu_hbm, wd_hbm,
    shg_hbm, shu_hbm, wsg_hbm, wsu_hbm, wsd_hbm, wo_hbm,
    hid_out, ctx_out,
    G, info, zs, A, Ts, Tr, Us, Ur, V, Z, far_s, near_s, y_s, far_r, near_r, y_r, H,
    wd, wgu, wsd, wo, sgate, sup, shg, shu, hid, gu, Pm, Wr, Lf, LT, Rk, own, ctx,
    ss, rs, ls,
):
    dp, z, t = lax.axis_index("dp"), lax.axis_index("expert"), lax.axis_index("tensor")
    ylo, core, x, yh = dp // 2, dp % 2, t // 2, t % 2
    xr, xl, xf = (x + 1) % 4, (x + 3) % 4, (x + 2) % 4
    yo = 1 - yh
    right, left, across = (dp, z, xr * 2 + yh), (dp, z, xl * 2 + yh), (dp, z, x * 2 + yo)
    sib = (ylo * 2 + 1 - core, z, t)
    opp = ((1 - ylo) * 2 + core, z, t)
    sib_dp, opp_dp, dia_dp = ylo * 2 + 1 - core, (1 - ylo) * 2 + core, (1 - ylo) * 2 + 1 - core

    count = [0]
    sent = []

    def send(src, dst, dev):
        i = count[0]
        count[0] += 1
        cp = pltpu.make_async_remote_copy(
            src_ref=src, dst_ref=dst, send_sem=ss.at[i], recv_sem=rs.at[i],
            device_id=dev, device_id_type=MESH,
        )
        cp.start()
        sent.append(cp)
        return cp

    locals_ = [0]

    def fetch(src, dst):
        i = locals_[0]
        locals_[0] += 1
        cp = pltpu.make_async_copy(src, dst, ls.at[i])
        cp.start()
        return cp

    tens = [(dx, dy) for dx in range(4) for dy in range(2) if dx or dy]

    own_in = [fetch(grad_ref.at[:, pl.ds(c * WIDTH, WIDTH)], G.at[c, t]) for c in range(CHUNKS)]
    barrier = pltpu.get_barrier_semaphore()
    peers = [(dp, z, ((x + dx) % 4) * 2 + (yh + dy) % 2) for dx, dy in tens]
    peers += [(dp, (z + dz) % 8, t) for dz in range(1, 8)]
    peers += [sib, opp]
    for p in peers:
        pl.semaphore_signal(barrier, inc=1, device_id=p, device_id_type=MESH)

    pend = dict(
        wd=fetch(wd_hbm, wd),
        wsd=fetch(wsd_hbm, wsd),
        wg=fetch(wg_hbm, wgu.at[pl.ds(0, FE)]),
        wu=fetch(wu_hbm, wgu.at[pl.ds(384, FE)]),
        wo=fetch(wo_hbm, wo),
        sgate=fetch(sgate_hbm, sgate),
        sup=fetch(sup_hbm, sup),
        shg=fetch(shg_hbm, shg),
        shu=fetch(shu_hbm, shu),
    )
    ws_in = []
    for c in range(CHUNKS):
        cols = pl.ds(c * WIDTH, WIDTH)
        ws_in.append(fetch(wsg_hbm.at[:, cols], Rk.at[c, pl.ds(ROWS, FS)]))
        ws_in.append(fetch(wsu_hbm.at[:, cols], Rk.at[c, pl.ds(ROWS + FS, FS)]))

    ids = ids_ref[...]
    gw = gw_ref[...]
    ov = ov_ref[...].astype(F32)
    experts = lax.broadcasted_iota(jnp.int32, (64, TOK), 0)
    oh = [(experts == ids[k : k + 1, :]).astype(F32) for k in range(2)]
    upper = lax.broadcasted_iota(jnp.int32, (TOK, TOK), 0) < lax.broadcasted_iota(
        jnp.int32, (TOK, TOK), 1
    )
    earlier = nn((oh[0] + oh[1]).astype(BF), upper.astype(F32).astype(BF))
    slots = [jnp.sum(earlier * oh[k], axis=0, keepdims=True) for k in range(2)]
    routed_weight = (gw * (1.0 - ov)).astype(BF).astype(F32)
    shared_weight = 1.0 + jnp.sum(gw * ov, axis=0, keepdims=True)
    info[t] = jnp.concatenate(
        [ids.astype(F32), slots[0], slots[1], routed_weight, shared_weight, shared_weight], axis=0
    )

    pl.semaphore_wait(barrier, len(peers))

    def gather0(buf, c):
        src = buf.at[c, t]
        return dict(
            y=send(src, src, across), r=send(src, src, right), l=send(src, src, left)
        )

    def gather1(buf, c, st):
        st["y"].wait_recv()
        src = buf.at[c, x * 2 + yo]
        st["pr"] = send(src, src, right)
        st["pl"] = send(src, src, left)

    def forward(buf, c, st, half):
        a = buf.at[c, xl * 2 + half, pl.ds(0, TOK // 2)]
        b = buf.at[c, xr * 2 + half, pl.ds(TOK // 2, TOK // 2)]
        st.setdefault("far", []).extend([send(a, a, right), send(b, b, left)])

    def gather2(buf, c, st):
        st["r"].wait_recv()
        st["l"].wait_recv()
        forward(buf, c, st, yh)

    def gather3(buf, c, st):
        st["pr"].wait_recv()
        st["pl"].wait_recv()
        forward(buf, c, st, yo)

    def gather4(buf, c, st):
        for cp in st["far"]:
            cp.wait_recv()

    def gather_all(buf):
        st = []
        for c in range(CHUNKS):
            st.append(gather0(buf, c))
        return st

    st = []
    own_in[0].wait()
    st.append(gather0(G, 0))
    infos = [send(info.at[t], info.at[t], p) for p in peers[: len(tens)]]
    for c in range(1, CHUNKS):
        own_in[c].wait()

    for cp in infos:
        cp.wait_recv()
    row_ids = lax.broadcasted_iota(jnp.int32, (ROWS, TOK), 0)
    weight = jnp.zeros((ROWS, 1), F32)
    Lf[...] = jnp.zeros_like(Lf)
    for b in range(8):
        part = info[b]
        hit = []
        for k in range(2):
            e = part[k : k + 1, :].astype(jnp.int32)
            j = part[2 + k : 3 + k, :].astype(jnp.int32)
            code = jnp.where(e % 8 == t, (e // 8) * PLANE + j * 8 + b, -1)
            on = (row_ids == code).astype(F32)
            weight = weight + jnp.sum(on * part[4 + k : 5 + k, :], axis=1, keepdims=True)
            hit.append(on)
        both = hit[0] + hit[1]
        Lf[0:ROWS, b * TOK : (b + 1) * TOK] = both
        Pm[:, b * TOK : (b + 1) * TOK] = both.astype(BF)
    Wr[...] = jnp.broadcast_to(weight, Wr.shape)

    def dispatch(c):
        got = nn(Pm[...], G[c].reshape(8 * TOK, WIDTH)) * Wr[:, 0:1]
        zs[c] = got.reshape(8, PLANE, WIDTH).astype(BF)
        A[c, dp, z] = zs[c, z]
        return [
            send(zs.at[c, (z + dz) % 8], A.at[c, dp, z], (dp, (z + dz) % 8, t))
            for dz in (1, 7, 2, 6, 3, 5, 4)
        ]

    gather1(G, 0, st[0])
    gather2(G, 0, st[0])
    for c in range(1, CHUNKS):
        st.append(gather0(G, c))
        gather3(G, c - 1, st[c - 1])
        gather1(G, c, st[c])
        gather4(G, c - 1, st[c - 1])
        if c == 1:
            zin = []
        zin.append(dispatch(c - 1))
        gather2(G, c, st[c])
    last = CHUNKS - 1
    gather3(G, last, st[last])
    gather4(G, last, st[last])
    zin.append(dispatch(last))

    pend["wsd"].wait()
    pend["shg"].wait()
    pend["shu"].wait()
    sw = jnp.concatenate([info[b, 6:7, :] for b in range(8)], axis=1)
    sh = jnp.zeros((FS, 8 * TOK), F32)
    for c in range(CHUNKS):
        sh = sh + nt(wsd[:, c * WIDTH : (c + 1) * WIDTH], G[c].reshape(8 * TOK, WIDTH))
    sg, su = swiglu_backward(sh * sw, shg[...].astype(F32), shu[...].astype(F32))
    Lf[ROWS : ROWS + FS, :] = sg
    Lf[ROWS + FS : ROWS + 2 * FS, :] = su
    for b in range(8):
        LT[b] = jnp.transpose(Lf[:, b * TOK : (b + 1) * TOK]).astype(BF)

    pend["wd"].wait()
    core_in, opp_in = [], []

    def spread(c):
        for cp in zin[c]:
            cp.wait_recv()
        opp_in.append(send(A.at[c, dp], A.at[c, dp], opp))
        core_in.append([send(A.at[c, dp], A.at[c, dp], sib)])

    def spread_on(c):
        opp_in[c].wait_recv()
        core_in[c].append(send(A.at[c, opp_dp], A.at[c, opp_dp], sib))

    def hidden_of(c, d):
        w = wd[:, c * WIDTH : (c + 1) * WIDTH]
        h = nt(rows_of(A[c, d]).astype(BF), w)
        if c == 0:
            hid[d] = h
        else:
            hid[d] = hid[d] + h

    spread(0)
    for c in range(1, CHUNKS):
        hidden_of(c - 1, dp)
        spread_on(c - 1)
        spread(c)
        hidden_of(c - 1, opp_dp)
        for cp in core_in[c - 1]:
            cp.wait_recv()
        hidden_of(c - 1, sib_dp)
        hidden_of(c - 1, dia_dp)
    hidden_of(last, dp)
    spread_on(last)
    pend["sgate"].wait()
    pend["sup"].wait()

    def act(d):
        h4 = hid[d].reshape(8, CAP, 8, FE)
        gs, us = [], []
        for j in range(CAP):
            g, u = swiglu_backward(
                h4[:, j],
                sgate[d, j].astype(F32).reshape(8, 8, FE),
                sup[d, j].astype(F32).reshape(8, 8, FE),
            )
            gs.append(g)
            us.append(u)
        gu[d, :, 0:FE] = jnp.stack(gs, axis=1).reshape(ROWS, FE).astype(BF)
        gu[d, :, 384 : 384 + FE] = jnp.stack(us, axis=1).reshape(ROWS, FE).astype(BF)

    gu[...] = jnp.zeros_like(gu)
    wgu[FE:384, :] = jnp.zeros((384 - FE, D), BF)
    wgu[384 + FE : DEPTH, :] = jnp.zeros((DEPTH - 384 - FE, D), BF)
    hidden_of(last, opp_dp)
    core_in[last][0].wait_recv()
    hidden_of(last, sib_dp)
    act(sib_dp)
    core_in[last][1].wait_recv()
    hidden_of(last, dia_dp)
    act(dia_dp)
    act(opp_dp)
    act(dp)

    pend["wg"].wait()
    pend["wu"].wait()

    def term(c, d):
        return nn(gu[d], wgu[:, c * WIDTH : (c + 1) * WIDTH])

    def planes(v):
        return v.reshape(8, PLANE, WIDTH).astype(BF)

    t_in, u_in, z_back = [], [], []
    for c in range(CHUNKS):
        Ts[c, 0] = planes(term(c, dia_dp))
        a = send(Ts.at[c, 0], Tr.at[c, 0], sib)
        Ts[c, 1] = planes(term(c, sib_dp))
        b = send(Ts.at[c, 1], Tr.at[c, 1], sib)
        t_in.append((a, b))
    for c in range(CHUNKS):
        v = term(c, opp_dp)
        t_in[c][0].wait_recv()
        Us[c] = planes(v + rows_of(Tr[c, 0]))
        u_in.append(send(Us.at[c], Ur.at[c], opp))
    for c in range(CHUNKS):
        v = term(c, dp)
        t_in[c][1].wait_recv()
        v = v + rows_of(Tr[c, 1])
        u_in[c].wait_recv()
        V[c] = planes(v + rows_of(Ur[c]))
        Z[c, z] = V[c, z]
        z_back.append([
            send(V.at[c, (z + dz) % 8], Z.at[c, z], (dp, (z + dz) % 8, t))
            for dz in (1, 7, 2, 6, 3, 5, 4)
        ])
    for cp in ws_in:
        cp.wait()

    def partial(c, place):
        w = LT[pl.ds(place * 2, 2)].reshape(2 * TOK, DEPTH)
        return nn(w, Rk[c]).reshape(2, TOK, WIDTH)

    half = TOK // 2
    fars, nears, ys = [], [], []

    def sum_far(c):
        for cp in z_back[c]:
            cp.wait_recv()
        Rk[c, 0:ROWS] = rows_of(Z[c]).astype(BF)
        Rk[c, ROWS + 2 * FS : DEPTH] = jnp.zeros((DEPTH - ROWS - 2 * FS, WIDTH), BF)
        v = partial(c, xf).astype(BF)
        far_s[c, 0] = v[:, 0:half]
        far_s[c, 1] = v[:, half:TOK]
        fars.append([
            send(far_s.at[c, 0], far_r.at[c, 0], right),
            send(far_s.at[c, 1], far_r.at[c, 1], left),
        ])

    def sum_near(c):
        a = partial(c, xr)
        b = partial(c, xl)
        fars[c][0].wait_recv()
        near_s[c, 0, :, 0:half] = (a[:, 0:half] + far_r[c, 0].astype(F32)).astype(BF)
        near_s[c, 0, :, half:TOK] = a[:, half:TOK].astype(BF)
        r = send(near_s.at[c, 0], near_r.at[c, 0], right)
        fars[c][1].wait_recv()
        near_s[c, 1, :, 0:half] = b[:, 0:half].astype(BF)
        near_s[c, 1, :, half:TOK] = (b[:, half:TOK] + far_r[c, 1].astype(F32)).astype(BF)
        l = send(near_s.at[c, 1], near_r.at[c, 1], left)
        nears.append((r, l))

    def sum_own(c):
        own[...] = partial(c, x)
        nears[c][0].wait_recv()
        nears[c][1].wait_recv()
        y_s[c] = (
            own[yo] + near_r[c, 0, yo].astype(F32) + near_r[c, 1, yo].astype(F32)
        ).astype(BF)
        ys.append(send(y_s.at[c], y_r.at[c], across))
        own[yh] = own[yh] + near_r[c, 0, yh].astype(F32) + near_r[c, 1, yh].astype(F32)

    def finish(c):
        ys[c].wait_recv()
        v = (own[yh] + y_r[c].astype(F32) + G[c, t].astype(F32)).astype(BF)
        H[c, t] = v
        hid_out[:, c * WIDTH : (c + 1) * WIDTH] = v

    hs = []
    sum_far(0)
    for c in range(CHUNKS):
        sum_near(c)
        if c + 1 < CHUNKS:
            sum_far(c + 1)
        sum_own(c)
        finish(c)
        hs.append(gather0(H, c))
    for c in range(CHUNKS):
        gather1(H, c, hs[c])
        gather2(H, c, hs[c])
    pend["wo"].wait()
    for c in range(CHUNKS):
        gather3(H, c, hs[c])
    for c in range(CHUNKS):
        gather4(H, c, hs[c])
        v = nt(H[c].reshape(8 * TOK, WIDTH), wo[:, c * WIDTH : (c + 1) * WIDTH])
        if c == 0:
            ctx[...] = v
        else:
            ctx[...] = ctx[...] + v
    ctx_out[...] = ctx[...].astype(BF)
    for cp in sent:
        cp.wait_send()


def body(
    grad_out, expert_ids, gate_weights, overflow, saved_gate, saved_up, w_gate, w_up, w_down,
    shared_gate_act, shared_up_act, ws_gate, ws_up, ws_down, w_out,
):
    anyspace = pl.BlockSpec(memory_space=pl.ANY)
    vmem = pl.BlockSpec(memory_space=pltpu.VMEM)
    C, W = CHUNKS, WIDTH
    scratch = [
        ((C, 8, TOK, W), BF),
        ((8, 8, TOK), F32),
        ((C, 8, PLANE, W), BF),
        ((C, 4, 8, PLANE, W), BF),
        ((C, 2, 8, PLANE, W), BF),
        ((C, 2, 8, PLANE, W), BF),
        ((C, 8, PLANE, W), BF),
        ((C, 8, PLANE, W), BF),
        ((C, 8, PLANE, W), BF),
        ((C, 8, PLANE, W), BF),
        ((C, 2, 2, TOK // 2, W), BF),
        ((C, 2, 2, TOK, W), BF),
        ((C, TOK, W), BF),
        ((C, 2, 2, TOK // 2, W), BF),
        ((C, 2, 2, TOK, W), BF),
        ((C, TOK, W), BF),
        ((C, 8, TOK, W), BF),
        ((FE, D), BF),
        ((DEPTH, D), BF),
        ((FS, D), BF),
        ((256, D), BF),
        ((4, CAP, 64, FE), BF),
        ((4, CAP, 64, FE), BF),
        ((FS, 8 * TOK), BF),
        ((FS, 8 * TOK), BF),
        ((4, ROWS, FE), F32),
        ((4, ROWS, DEPTH), BF),
        ((ROWS, 8 * TOK), BF),
        ((ROWS, TOK), F32),
        ((DEPTH, 8 * TOK), F32),
        ((8, TOK, DEPTH), BF),
        ((C, DEPTH, W), BF),
        ((2, TOK, W), F32),
        ((8 * TOK, 256), F32),
    ]
    return pl.pallas_call(
        kernel,
        out_shape=(
            jax.ShapeDtypeStruct((TOK, D), BF),
            jax.ShapeDtypeStruct((8 * TOK, 256), BF),
        ),
        in_specs=[anyspace, vmem, vmem, vmem] + [anyspace] * 11,
        out_specs=(vmem, vmem),
        scratch_shapes=[pltpu.VMEM(s, d) for s, d in scratch]
        + [pltpu.SemaphoreType.DMA((N_SEM,))] * 2
        + [pltpu.SemaphoreType.DMA((32,))],
        compiler_params=pltpu.CompilerParams(
            collective_id=0, has_side_effects=True, vmem_limit_bytes=63 * 1024 * 1024
        ),
        name="layer",
    )(
        grad_out,
        expert_ids.T,
        gate_weights.T,
        overflow.T,
        saved_gate[0].transpose(0, 2, 1, 3),
        saved_up[0].transpose(0, 2, 1, 3),
        w_gate[0].T,
        w_up[0].T,
        w_down[0],
        shared_gate_act.T,
        shared_up_act.T,
        ws_gate.T,
        ws_up.T,
        ws_down,
        w_out,
    )


def solution(mesh):
    in_specs = (
        P(("dp", "expert", "tensor"), None),
        P(("dp", "expert", "tensor"), None),
        P(("dp", "expert", "tensor"), None),
        P(("dp", "expert", "tensor"), None),
        P(("expert", "tensor"), None, None, None, "dp"),
        P(("expert", "tensor"), None, None, None, "dp"),
        P(("expert", "tensor"), None, "dp"),
        P(("expert", "tensor"), None, "dp"),
        P(("expert", "tensor"), "dp", None),
        P(("dp", "expert"), "tensor"),
        P(("dp", "expert"), "tensor"),
        P(None, "tensor"),
        P(None, "tensor"),
        P("tensor", None),
        P("tensor", None),
    )
    out_specs = (P(("dp", "expert", "tensor"), None), P(("dp", "expert"), "tensor"))
    return jax.shard_map(body, mesh=mesh, in_specs=in_specs, out_specs=out_specs, check_vma=False)
```

```python
import functools

import jax
import jax.numpy as jnp
from jax import lax
from jax.experimental import pallas as pl
from jax.experimental.pallas import tpu as pltpu
from jax.sharding import PartitionSpec as P

MESH = pl.DeviceIdType.MESH
BF = jnp.bfloat16
F32 = jnp.float32
CHUNKS = 4
TOK = 128
D = 2048
WIDTH = D // CHUNKS
CAP = 5
PLANE = CAP * 8
ROWS = 8 * PLANE
FE = 352
FS = 176
DEPTH = 768
N_SEM = 200
HALF = TOK // 2


def nn(a, b):
    return jnp.dot(a, b, preferred_element_type=F32)


def nt(a, b):
    return lax.dot_general(a, b, (((1,), (1,)), ((), ())), preferred_element_type=F32)


def swiglu_backward(hidden, gate_act, up_act):
    s = jax.nn.sigmoid(gate_act)
    gate = hidden * up_act * s * (1.0 + gate_act * (1.0 - s))
    up = hidden * gate_act * s
    return gate, up


def rows_of(planes):
    return planes.astype(F32).reshape(ROWS, planes.shape[-1])


def kernel(
    grad_ref, ids_ref, gw_ref, ov_ref, sgate_hbm, sup_hbm, wg_hbm, wu_hbm, wd_hbm,
    shg_hbm, shu_hbm, wsg_hbm, wsu_hbm, wsd_hbm, wo_hbm,
    hid_out, ctx_out,
    G, info, zs, A, Ts, Tr, Us, Ur, V, Z, far_s, near_s, y_s, far_r, near_r, y_r, W,
    wd, wgu, wsd, sgate, sup, shg, shu, hid, gu, Pm, Wr, Lf, LT, Rk, own, ctx, ctx_s, ctx_r,
    ss, rs, ls,
):
    dp, z, t = lax.axis_index("dp"), lax.axis_index("expert"), lax.axis_index("tensor")
    ylo, core, x, yh = dp // 2, dp % 2, t // 2, t % 2
    xr, xl, xf = (x + 1) % 4, (x + 3) % 4, (x + 2) % 4
    yo = 1 - yh
    right, left, across = (dp, z, xr * 2 + yh), (dp, z, xl * 2 + yh), (dp, z, x * 2 + yo)
    sib = (ylo * 2 + 1 - core, z, t)
    opp = ((1 - ylo) * 2 + core, z, t)
    sib_dp, opp_dp, dia_dp = ylo * 2 + 1 - core, (1 - ylo) * 2 + core, (1 - ylo) * 2 + 1 - core

    count = [0]
    sent = []

    def send(src, dst, dev):
        i = count[0]
        count[0] += 1
        cp = pltpu.make_async_remote_copy(
            src_ref=src, dst_ref=dst, send_sem=ss.at[i], recv_sem=rs.at[i],
            device_id=dev, device_id_type=MESH,
        )
        cp.start()
        sent.append(cp)
        return cp

    locals_ = [0]

    def fetch(src, dst):
        i = locals_[0]
        locals_[0] += 1
        cp = pltpu.make_async_copy(src, dst, ls.at[i])
        cp.start()
        return cp

    tens = [(dx, dy) for dx in range(4) for dy in range(2) if dx or dy]

    own_in = [fetch(grad_ref.at[:, pl.ds(c * WIDTH, WIDTH)], G.at[c, t]) for c in range(CHUNKS)]
    barrier = pltpu.get_barrier_semaphore()
    peers = [(dp, z, ((x + dx) % 4) * 2 + (yh + dy) % 2) for dx, dy in tens]
    peers += [(dp, (z + dz) % 8, t) for dz in range(1, 8)]
    peers += [sib, opp]
    for p in peers:
        pl.semaphore_signal(barrier, inc=1, device_id=p, device_id_type=MESH)

    pend = dict(
        wd=fetch(wd_hbm, wd),
        wsd=fetch(wsd_hbm, wsd),
        wg=fetch(wg_hbm, wgu.at[pl.ds(0, FE)]),
        wu=fetch(wu_hbm, wgu.at[pl.ds(384, FE)]),
        wo=fetch(
            wo_hbm.at[pl.ds(pl.multiple_of(core * TOK, TOK), TOK)],
            W.at[t, pl.ds(pl.multiple_of(core * TOK, TOK), TOK)],
        ),
        sgate=fetch(sgate_hbm, sgate),
        sup=fetch(sup_hbm, sup),
        shg=fetch(shg_hbm, shg),
        shu=fetch(shu_hbm, shu),
    )
    ws_in = []
    for c in range(CHUNKS):
        cols = pl.ds(c * WIDTH, WIDTH)
        ws_in.append(fetch(wsg_hbm.at[:, cols], Rk.at[c, pl.ds(ROWS, FS)]))
        ws_in.append(fetch(wsu_hbm.at[:, cols], Rk.at[c, pl.ds(ROWS + FS, FS)]))

    ids = ids_ref[...]
    gw = gw_ref[...]
    ov = ov_ref[...].astype(F32)
    experts = lax.broadcasted_iota(jnp.int32, (64, TOK), 0)
    oh = [(experts == ids[k : k + 1, :]).astype(F32) for k in range(2)]
    upper = lax.broadcasted_iota(jnp.int32, (TOK, TOK), 0) < lax.broadcasted_iota(
        jnp.int32, (TOK, TOK), 1
    )
    earlier = nn((oh[0] + oh[1]).astype(BF), upper.astype(F32).astype(BF))
    slots = [jnp.sum(earlier * oh[k], axis=0, keepdims=True) for k in range(2)]
    routed_weight = (gw * (1.0 - ov)).astype(BF).astype(F32)
    shared_weight = 1.0 + jnp.sum(gw * ov, axis=0, keepdims=True)
    info[t] = jnp.concatenate(
        [ids.astype(F32), slots[0], slots[1], routed_weight, shared_weight, shared_weight], axis=0
    )

    pl.semaphore_wait(barrier, len(peers))

    def block_of_tokens(c):
        def view(i, part=None):
            return G.at[c, i] if part is None else G.at[c, i, pl.ds(part * HALF, HALF)]

        return view

    def block_of_w(i, part=None):
        if part is None:
            return W.at[i, pl.ds(pl.multiple_of(core * TOK, TOK), TOK)]
        return W.at[i, pl.ds(pl.multiple_of(core * TOK + part * HALF, HALF), HALF)]

    def gather_y(view):
        return dict(view=view, y=send(view(t), view(t), across), far=[])

    def gather_x(g):
        src = g["view"](t)
        g["near"] = [send(src, src, right), send(src, src, left)]

    def gather_partner(g):
        g["y"].wait_recv()
        src = g["view"](x * 2 + yo)
        g["partner"] = [send(src, src, right), send(src, src, left)]

    def forward(g, kind, half):
        for cp in g[kind]:
            cp.wait_recv()
        a = g["view"](xl * 2 + half, 0)
        b = g["view"](xr * 2 + half, 1)
        g["far"] += [send(a, a, right), send(b, b, left)]

    def gather_far(g):
        for cp in g["far"]:
            cp.wait_recv()

    gs = []
    for c in range(CHUNKS):
        own_in[c].wait()
        gs.append(gather_y(block_of_tokens(c)))
        if c < 2:
            gather_x(gs[c])
        if c == 0:
            infos = [send(info.at[t], info.at[t], p) for p in peers[: len(tens)]]
    gather_partner(gs[0])

    for cp in infos:
        cp.wait_recv()
    row_ids = lax.broadcasted_iota(jnp.int32, (ROWS, TOK), 0)
    weight = jnp.zeros((ROWS, 1), F32)
    Lf[...] = jnp.zeros_like(Lf)
    for b in range(8):
        part = info[b]
        hit = []
        for k in range(2):
            e = part[k : k + 1, :].astype(jnp.int32)
            j = part[2 + k : 3 + k, :].astype(jnp.int32)
            code = jnp.where(e % 8 == t, (e // 8) * PLANE + j * 8 + b, -1)
            on = (row_ids == code).astype(F32)
            weight = weight + jnp.sum(on * part[4 + k : 5 + k, :], axis=1, keepdims=True)
            hit.append(on)
        both = hit[0] + hit[1]
        Lf[0:ROWS, b * TOK : (b + 1) * TOK] = both
        Pm[:, b * TOK : (b + 1) * TOK] = both.astype(BF)
    Wr[...] = jnp.broadcast_to(weight, Wr.shape)

    def dispatch(c):
        got = nn(Pm[...], G[c].reshape(8 * TOK, WIDTH)) * Wr[:, 0:1]
        zs[c] = got.reshape(8, PLANE, WIDTH).astype(BF)
        A[c, dp, z] = zs[c, z]
        return [
            send(zs.at[c, (z + dz) % 8], A.at[c, dp, z], (dp, (z + dz) % 8, t))
            for dz in (1, 7, 2, 6, 3, 5, 4)
        ]

    zin, core_in, opp_in = [], [], []
    last = CHUNKS - 1

    def spread(c):
        for cp in zin[c]:
            cp.wait_recv()
        opp_in.append(send(A.at[c, dp], A.at[c, dp], opp))
        core_in.append([send(A.at[c, dp], A.at[c, dp], sib)])

    def spread_on(c):
        opp_in[c].wait_recv()
        core_in[c].append(send(A.at[c, opp_dp], A.at[c, opp_dp], sib))

    def hidden_of(c, d):
        w = wd[:, c * WIDTH : (c + 1) * WIDTH]
        h = nt(rows_of(A[c, d]).astype(BF), w)
        if c == 0:
            hid[d] = h
        else:
            hid[d] = hid[d] + h

    def hidden_all(c):
        hidden_of(c, dp)
        hidden_of(c, opp_dp)
        for cp in core_in[c]:
            cp.wait_recv()
        hidden_of(c, sib_dp)
        hidden_of(c, dia_dp)

    for k in range(CHUNKS):
        forward(gs[k], "near", yh)
        if k + 1 < CHUNKS:
            gather_partner(gs[k + 1])
        forward(gs[k], "partner", yo)
        if k + 2 < CHUNKS:
            gather_x(gs[k + 2])
        gather_far(gs[k])
        zin.append(dispatch(k))
        if k >= 1:
            spread(k - 1)
        if k >= 2:
            spread_on(k - 2)
        if k == 2:
            pend["wd"].wait()
        if k >= 3:
            hidden_all(k - 3)
    pend["wo"].wait()
    gw_ = gather_y(block_of_w)
    gather_x(gw_)

    pend["wsd"].wait()
    pend["shg"].wait()
    pend["shu"].wait()
    sw = jnp.concatenate([info[b, 6:7, :] for b in range(8)], axis=1)
    sh = jnp.zeros((FS, 8 * TOK), F32)
    for c in range(CHUNKS):
        sh = sh + nt(wsd[:, c * WIDTH : (c + 1) * WIDTH], G[c].reshape(8 * TOK, WIDTH))
    sg, su = swiglu_backward(sh * sw, shg[...].astype(F32), shu[...].astype(F32))
    Lf[ROWS : ROWS + FS, :] = sg
    Lf[ROWS + FS : ROWS + 2 * FS, :] = su
    for b in range(8):
        LT[b] = jnp.transpose(Lf[:, b * TOK : (b + 1) * TOK]).astype(BF)

    spread(last)
    spread_on(last - 1)
    if last >= 2:
        hidden_all(last - 2)
    gather_partner(gw_)
    forward(gw_, "near", yh)
    hidden_all(last - 1)
    hidden_of(last, dp)
    spread_on(last)
    pend["sgate"].wait()
    pend["sup"].wait()

    def act(d):
        h4 = hid[d].reshape(8, CAP, 8, FE)
        gs, us = [], []
        for j in range(CAP):
            g, u = swiglu_backward(
                h4[:, j],
                sgate[d, j].astype(F32).reshape(8, 8, FE),
                sup[d, j].astype(F32).reshape(8, 8, FE),
            )
            gs.append(g)
            us.append(u)
        gu[d, :, 0:FE] = jnp.stack(gs, axis=1).reshape(ROWS, FE).astype(BF)
        gu[d, :, 384 : 384 + FE] = jnp.stack(us, axis=1).reshape(ROWS, FE).astype(BF)

    gu[...] = jnp.zeros_like(gu)
    wgu[FE:384, :] = jnp.zeros((384 - FE, D), BF)
    wgu[384 + FE : DEPTH, :] = jnp.zeros((DEPTH - 384 - FE, D), BF)
    hidden_of(last, opp_dp)
    core_in[last][0].wait_recv()
    hidden_of(last, sib_dp)
    act(sib_dp)
    core_in[last][1].wait_recv()
    hidden_of(last, dia_dp)
    act(dia_dp)
    act(opp_dp)
    act(dp)

    forward(gw_, "partner", yo)

    pend["wg"].wait()
    pend["wu"].wait()

    def term(c, d):
        return nn(gu[d], wgu[:, c * WIDTH : (c + 1) * WIDTH])

    def planes(v):
        return v.reshape(8, PLANE, WIDTH).astype(BF)

    t_in, u_in, z_back = [], [], []

    def sum_core(c):
        Ts[c, 0] = planes(term(c, dia_dp))
        a = send(Ts.at[c, 0], Tr.at[c, 0], sib)
        Ts[c, 1] = planes(term(c, sib_dp))
        b = send(Ts.at[c, 1], Tr.at[c, 1], sib)
        t_in.append((a, b))

    def sum_opp(c):
        v = term(c, opp_dp)
        t_in[c][0].wait_recv()
        Us[c] = planes(v + rows_of(Tr[c, 0]))
        u_in.append(send(Us.at[c], Ur.at[c], opp))

    def sum_dp(c):
        v = term(c, dp)
        t_in[c][1].wait_recv()
        v = v + rows_of(Tr[c, 1])
        u_in[c].wait_recv()
        V[c] = planes(v + rows_of(Ur[c]))
        Z[c, z] = V[c, z]
        z_back.append([
            send(V.at[c, (z + dz) % 8], Z.at[c, z], (dp, (z + dz) % 8, t))
            for dz in (1, 7, 2, 6, 3, 5, 4)
        ])

    def partial(c, place):
        w = LT[pl.ds(place * 2, 2)].reshape(2 * TOK, DEPTH)
        return nn(w, Rk[c]).reshape(2, TOK, WIDTH)

    fars, nears, ys = [], [], []

    def sum_far(c):
        for cp in z_back[c]:
            cp.wait_recv()
        Rk[c, 0:ROWS] = rows_of(Z[c]).astype(BF)
        v = partial(c, xf).astype(BF)
        far_s[c, 0] = v[:, 0:HALF]
        far_s[c, 1] = v[:, HALF:TOK]
        fars.append([
            send(far_s.at[c, 0], far_r.at[c, 0], right),
            send(far_s.at[c, 1], far_r.at[c, 1], left),
        ])

    def sum_near(c):
        a = partial(c, xr)
        b = partial(c, xl)
        fars[c][0].wait_recv()
        near_s[c, 0, :, 0:HALF] = (a[:, 0:HALF] + far_r[c, 0].astype(F32)).astype(BF)
        near_s[c, 0, :, HALF:TOK] = a[:, HALF:TOK].astype(BF)
        r = send(near_s.at[c, 0], near_r.at[c, 0], right)
        fars[c][1].wait_recv()
        near_s[c, 1, :, 0:HALF] = b[:, 0:HALF].astype(BF)
        near_s[c, 1, :, HALF:TOK] = (b[:, HALF:TOK] + far_r[c, 1].astype(F32)).astype(BF)
        l = send(near_s.at[c, 1], near_r.at[c, 1], left)
        nears.append((r, l))

    def sum_own(c):
        mine = own.at[c % 2]
        mine[...] = partial(c, x)
        nears[c][0].wait_recv()
        nears[c][1].wait_recv()
        y_s[c] = (
            mine[yo] + near_r[c, 0, yo].astype(F32) + near_r[c, 1, yo].astype(F32)
        ).astype(BF)
        ys.append(send(y_s.at[c], y_r.at[c], across))
        mine[yh] = mine[yh] + near_r[c, 0, yh].astype(F32) + near_r[c, 1, yh].astype(F32)

    def finish(c):
        cols = slice(c * WIDTH, (c + 1) * WIDTH)
        ys[c].wait_recv()
        v = (own[c % 2, yh] + y_r[c].astype(F32) + G[c, t].astype(F32)).astype(BF)
        hid_out[:, cols] = v
        w = nt(v, W[:, :, cols].reshape(D, WIDTH))
        if c == 0:
            ctx[...] = w
        else:
            ctx[...] = ctx[...] + w

    sum_core(0)
    for k in range(CHUNKS + 5):
        if k + 1 < CHUNKS:
            sum_core(k + 1)
        if k == CHUNKS - 1:
            gather_far(gw_)
            mine = W.at[:, pl.ds(pl.multiple_of(core * TOK, TOK), TOK)]
            w_in = send(mine, mine, sib)
        if k < CHUNKS:
            sum_opp(k)
        if 0 <= k - 1 < CHUNKS:
            sum_dp(k - 1)
        if k == 1:
            for cp in ws_in:
                cp.wait()
            for c in range(CHUNKS):
                Rk[c, ROWS + 2 * FS : DEPTH] = jnp.zeros((DEPTH - ROWS - 2 * FS, WIDTH), BF)
        if k == CHUNKS:
            pass
        if 0 <= k - 2 < CHUNKS:
            sum_far(k - 2)
        if 0 <= k - 3 < CHUNKS:
            sum_near(k - 3)
        if k == CHUNKS:
            w_in.wait_recv()
        if 0 <= k - 5 < CHUNKS:
            finish(k - 5)
        if 0 <= k - 4 < CHUNKS:
            sum_own(k - 4)
    for b in range(8):
        ctx_s[b] = ctx[:, b * 256 : (b + 1) * 256].astype(BF)
    outs = [
        send(ctx_s.at[p[2]], ctx_r.at[t], p) for p in peers[: len(tens)]
    ]
    ctx_r[t] = ctx_s[t]
    for cp in outs:
        cp.wait_recv()
    ctx_out[...] = ctx_r[...].reshape(8 * TOK, 256)
    for cp in sent:
        cp.wait_send()


def body(
    grad_out, expert_ids, gate_weights, overflow, saved_gate, saved_up, w_gate, w_up, w_down,
    shared_gate_act, shared_up_act, ws_gate, ws_up, ws_down, w_out,
):
    anyspace = pl.BlockSpec(memory_space=pl.ANY)
    vmem = pl.BlockSpec(memory_space=pltpu.VMEM)
    C, W = CHUNKS, WIDTH
    scratch = [
        ((C, 8, TOK, W), BF),
        ((8, 8, TOK), F32),
        ((C, 8, PLANE, W), BF),
        ((C, 4, 8, PLANE, W), BF),
        ((C, 2, 8, PLANE, W), BF),
        ((C, 2, 8, PLANE, W), BF),
        ((C, 8, PLANE, W), BF),
        ((C, 8, PLANE, W), BF),
        ((C, 8, PLANE, W), BF),
        ((C, 8, PLANE, W), BF),
        ((C, 2, 2, TOK // 2, W), BF),
        ((C, 2, 2, TOK, W), BF),
        ((C, TOK, W), BF),
        ((C, 2, 2, TOK // 2, W), BF),
        ((C, 2, 2, TOK, W), BF),
        ((C, TOK, W), BF),
        ((8, 256, D), BF),
        ((FE, D), BF),
        ((DEPTH, D), BF),
        ((FS, D), BF),
        ((4, CAP, 64, FE), BF),
        ((4, CAP, 64, FE), BF),
        ((FS, 8 * TOK), BF),
        ((FS, 8 * TOK), BF),
        ((4, ROWS, FE), F32),
        ((4, ROWS, DEPTH), BF),
        ((ROWS, 8 * TOK), BF),
        ((ROWS, TOK), F32),
        ((DEPTH, 8 * TOK), F32),
        ((8, TOK, DEPTH), BF),
        ((C, DEPTH, W), BF),
        ((2, 2, TOK, W), F32),
        ((TOK, D), F32),
        ((8, TOK, 256), BF),
        ((8, TOK, 256), BF),
    ]
    return pl.pallas_call(
        kernel,
        out_shape=(
            jax.ShapeDtypeStruct((TOK, D), BF),
            jax.ShapeDtypeStruct((8 * TOK, 256), BF),
        ),
        in_specs=[anyspace, vmem, vmem, vmem] + [anyspace] * 11,
        out_specs=(vmem, vmem),
        scratch_shapes=[pltpu.VMEM(s, d) for s, d in scratch]
        + [pltpu.SemaphoreType.DMA((N_SEM,))] * 2
        + [pltpu.SemaphoreType.DMA((32,))],
        compiler_params=pltpu.CompilerParams(
            collective_id=0, has_side_effects=True, vmem_limit_bytes=63 * 1024 * 1024
        ),
        name="layer",
    )(
        grad_out,
        expert_ids.T,
        gate_weights.T,
        overflow.T,
        saved_gate[0].transpose(0, 2, 1, 3),
        saved_up[0].transpose(0, 2, 1, 3),
        w_gate[0].T,
        w_up[0].T,
        w_down[0],
        shared_gate_act.T,
        shared_up_act.T,
        ws_gate.T,
        ws_up.T,
        ws_down,
        w_out,
    )


def solution(mesh):
    in_specs = (
        P(("dp", "expert", "tensor"), None),
        P(("dp", "expert", "tensor"), None),
        P(("dp", "expert", "tensor"), None),
        P(("dp", "expert", "tensor"), None),
        P(("expert", "tensor"), None, None, None, "dp"),
        P(("expert", "tensor"), None, None, None, "dp"),
        P(("expert", "tensor"), None, "dp"),
        P(("expert", "tensor"), None, "dp"),
        P(("expert", "tensor"), "dp", None),
        P(("dp", "expert"), "tensor"),
        P(("dp", "expert"), "tensor"),
        P(None, "tensor"),
        P(None, "tensor"),
        P("tensor", None),
        P("tensor", None),
    )
    out_specs = (P(("dp", "expert", "tensor"), None), P(("dp", "expert"), "tensor"))
    return jax.shard_map(body, mesh=mesh, in_specs=in_specs, out_specs=out_specs, check_vma=False)
```

```python
import functools

import jax
import jax.numpy as jnp
from jax import lax
from jax.experimental import pallas as pl
from jax.experimental.pallas import tpu as pltpu
from jax.sharding import PartitionSpec as P

MESH = pl.DeviceIdType.MESH
BF = jnp.bfloat16
F32 = jnp.float32
CHUNKS = 4
TOK = 128
D = 2048
WIDTH = D // CHUNKS
CAP = 5
PLANE = CAP * 8
ROWS = 8 * PLANE
FE = 352
FS = 176
DEPTH = 768
N_SEM = 260
HALF = TOK // 2


def nn(a, b):
    return jnp.dot(a, b, preferred_element_type=F32)


def nt(a, b):
    return lax.dot_general(a, b, (((1,), (1,)), ((), ())), preferred_element_type=F32)


def swiglu_backward(hidden, gate_act, up_act):
    s = jax.nn.sigmoid(gate_act)
    gate = hidden * up_act * s * (1.0 + gate_act * (1.0 - s))
    up = hidden * gate_act * s
    return gate, up


def rows_of(planes):
    return planes.astype(F32).reshape(ROWS, planes.shape[-1])


def kernel(
    grad_ref, ids_ref, gw_ref, ov_ref, sgate_hbm, sup_hbm, wg_hbm, wu_hbm, wd_hbm,
    shg_hbm, shu_hbm, wsg_hbm, wsu_hbm, wsd_hbm, wo_hbm,
    hid_out, ctx_out,
    G, info, zs, A, Ts, Tr, Us, Ur, V, Z, far_s, near_s, y_s, far_r, near_r, y_r, W,
    wd, wgu, wsd, sgate, sup, shg, shu, hid, gu, Xs, Xr, Q, Lf, LT, Rk, own, ctx, ctx_s, ctx_r,
    ss, rs, ls,
):
    dp, z, t = lax.axis_index("dp"), lax.axis_index("expert"), lax.axis_index("tensor")
    ylo, core, x, yh = dp // 2, dp % 2, t // 2, t % 2
    xr, xl, xf = (x + 1) % 4, (x + 3) % 4, (x + 2) % 4
    yo = 1 - yh
    right, left, across = (dp, z, xr * 2 + yh), (dp, z, xl * 2 + yh), (dp, z, x * 2 + yo)
    sib = (ylo * 2 + 1 - core, z, t)
    opp = ((1 - ylo) * 2 + core, z, t)
    sib_dp, opp_dp, dia_dp = ylo * 2 + 1 - core, (1 - ylo) * 2 + core, (1 - ylo) * 2 + 1 - core

    count = [0]
    sent = []

    def send(src, dst, dev):
        i = count[0]
        count[0] += 1
        cp = pltpu.make_async_remote_copy(
            src_ref=src, dst_ref=dst, send_sem=ss.at[i], recv_sem=rs.at[i],
            device_id=dev, device_id_type=MESH,
        )
        cp.start()
        sent.append(cp)
        return cp

    locals_ = [0]

    def fetch(src, dst):
        i = locals_[0]
        locals_[0] += 1
        cp = pltpu.make_async_copy(src, dst, ls.at[i])
        cp.start()
        return cp

    tens = [(dx, dy) for dx in range(4) for dy in range(2) if dx or dy]

    own_in = [fetch(grad_ref.at[:, pl.ds(c * WIDTH, WIDTH)], G.at[c, t]) for c in range(CHUNKS)]
    barrier = pltpu.get_barrier_semaphore()
    peers = [(dp, z, ((x + dx) % 4) * 2 + (yh + dy) % 2) for dx, dy in tens]
    peers += [(dp, (z + dz) % 8, t) for dz in range(1, 8)]
    peers += [sib, opp]
    for p in peers:
        pl.semaphore_signal(barrier, inc=1, device_id=p, device_id_type=MESH)

    pend = dict(
        wd=fetch(wd_hbm, wd),
        wsd=fetch(wsd_hbm, wsd),
        wg=fetch(wg_hbm, wgu.at[pl.ds(0, FE)]),
        wu=fetch(wu_hbm, wgu.at[pl.ds(384, FE)]),
        wo=fetch(
            wo_hbm.at[pl.ds(pl.multiple_of(core * TOK, TOK), TOK)],
            W.at[t, pl.ds(pl.multiple_of(core * TOK, TOK), TOK)],
        ),
        sgate=fetch(sgate_hbm, sgate),
        sup=fetch(sup_hbm, sup),
        shg=fetch(shg_hbm, shg),
        shu=fetch(shu_hbm, shu),
    )
    ws_in = []
    for c in range(CHUNKS):
        cols = pl.ds(c * WIDTH, WIDTH)
        ws_in.append(fetch(wsg_hbm.at[:, cols], Rk.at[c, pl.ds(ROWS, FS)]))
        ws_in.append(fetch(wsu_hbm.at[:, cols], Rk.at[c, pl.ds(ROWS + FS, FS)]))

    ids = ids_ref[...]
    gw = gw_ref[...]
    ov = ov_ref[...].astype(F32)
    experts = lax.broadcasted_iota(jnp.int32, (64, TOK), 0)
    oh = [(experts == ids[k : k + 1, :]).astype(F32) for k in range(2)]
    upper = lax.broadcasted_iota(jnp.int32, (TOK, TOK), 0) < lax.broadcasted_iota(
        jnp.int32, (TOK, TOK), 1
    )
    earlier = nn((oh[0] + oh[1]).astype(BF), upper.astype(F32).astype(BF))
    slots = [jnp.sum(earlier * oh[k], axis=0, keepdims=True) for k in range(2)]
    routed_weight = (gw * (1.0 - ov)).astype(BF).astype(F32)
    shared_weight = 1.0 + jnp.sum(gw * ov, axis=0, keepdims=True)
    info[t] = jnp.concatenate(
        [ids.astype(F32), slots[0], slots[1], routed_weight, shared_weight, shared_weight], axis=0
    )

    row_ids = lax.broadcasted_iota(jnp.int32, (ROWS, TOK), 0)
    weight = jnp.zeros((ROWS, 1), F32)
    pick = jnp.zeros((ROWS, TOK), F32)
    for k in range(2):
        e = ids[k : k + 1, :]
        code = (e % 8) * PLANE + (e // 8) * CAP + slots[k].astype(jnp.int32)
        on = (row_ids == code).astype(F32)
        weight = weight + jnp.sum(on * routed_weight[k : k + 1, :], axis=1, keepdims=True)
        pick = pick + on
    pick = pick.astype(BF)
    r = lax.broadcasted_iota(jnp.int32, (ROWS, ROWS), 0)
    from_row = (r % 8) * PLANE + (r // PLANE) * CAP + (r % PLANE) // 8
    Q[...] = (lax.broadcasted_iota(jnp.int32, (ROWS, ROWS), 1) == from_row).astype(F32).astype(BF)
    for c in range(CHUNKS):
        own_in[c].wait()
        Xs[c] = (nn(pick, G[c, t]) * weight).reshape(8, PLANE, WIDTH).astype(BF)
        Xr[c, t] = Xs[c, t]

    pl.semaphore_wait(barrier, len(peers))

    def block_of_tokens(c):
        def view(i, part=None):
            return G.at[c, i] if part is None else G.at[c, i, pl.ds(part * HALF, HALF)]

        return view

    def block_of_w(i, part=None):
        if part is None:
            return W.at[i, pl.ds(pl.multiple_of(core * TOK, TOK), TOK)]
        return W.at[i, pl.ds(pl.multiple_of(core * TOK + part * HALF, HALF), HALF)]

    def gather_y(view):
        return dict(view=view, y=send(view(t), view(t), across), far=[])

    def gather_x(g):
        src = g["view"](t)
        g["near"] = [send(src, src, right), send(src, src, left)]

    def gather_partner(g):
        g["y"].wait_recv()
        src = g["view"](x * 2 + yo)
        g["partner"] = [send(src, src, right), send(src, src, left)]

    def forward(g, kind, half):
        for cp in g[kind]:
            cp.wait_recv()
        a = g["view"](xl * 2 + half, 0)
        b = g["view"](xr * 2 + half, 1)
        g["far"] += [send(a, a, right), send(b, b, left)]

    def gather_far(g):
        for cp in g["far"]:
            cp.wait_recv()

    x_in = []
    for c in range(CHUNKS):
        x_in.append([send(Xs.at[c, p[2]], Xr.at[c, t], p) for p in peers[: len(tens)]])
        if c == 1:
            infos = [send(info.at[t], info.at[t], p) for p in peers[: len(tens)]]
    gs = [gather_y(block_of_tokens(c)) for c in range(CHUNKS)]
    gather_x(gs[0])

    def dispatch(c):
        for cp in x_in[c]:
            cp.wait_recv()
        zs[c] = nn(Q[...], rows_of(Xr[c]).astype(BF)).reshape(8, PLANE, WIDTH).astype(BF)
        A[c, dp, z] = zs[c, z]
        return [
            send(zs.at[c, (z + dz) % 8], A.at[c, dp, z], (dp, (z + dz) % 8, t))
            for dz in (1, 7, 2, 6, 3, 5, 4)
        ]

    zin, core_in, opp_in = [], [], []
    last = CHUNKS - 1

    def spread(c):
        for cp in zin[c]:
            cp.wait_recv()
        opp_in.append(send(A.at[c, dp], A.at[c, dp], opp))
        core_in.append([send(A.at[c, dp], A.at[c, dp], sib)])

    def spread_on(c):
        opp_in[c].wait_recv()
        core_in[c].append(send(A.at[c, opp_dp], A.at[c, opp_dp], sib))

    def hidden_of(c, d):
        w = wd[:, c * WIDTH : (c + 1) * WIDTH]
        h = nt(rows_of(A[c, d]).astype(BF), w)
        if c == 0:
            hid[d] = h
        else:
            hid[d] = hid[d] + h

    def hidden_all(c):
        hidden_of(c, dp)
        hidden_of(c, opp_dp)
        for cp in core_in[c]:
            cp.wait_recv()
        hidden_of(c, sib_dp)
        hidden_of(c, dia_dp)

    def act(d):
        h4 = hid[d].reshape(8, CAP, 8, FE)
        gs, us = [], []
        for j in range(CAP):
            g, u = swiglu_backward(
                h4[:, j],
                sgate[d, j].astype(F32).reshape(8, 8, FE),
                sup[d, j].astype(F32).reshape(8, 8, FE),
            )
            gs.append(g)
            us.append(u)
        gu[d, :, 0:FE] = jnp.stack(gs, axis=1).reshape(ROWS, FE).astype(BF)
        gu[d, :, 384 : 384 + FE] = jnp.stack(us, axis=1).reshape(ROWS, FE).astype(BF)

    def shared_units():
        for cp in infos:
            cp.wait_recv()
        row_ids = lax.broadcasted_iota(jnp.int32, (ROWS, TOK), 0)
        Lf[ROWS + 2 * FS : DEPTH, :] = jnp.zeros((DEPTH - ROWS - 2 * FS, 8 * TOK), F32)
        for b in range(8):
            part = info[b]
            hit = []
            for k in range(2):
                e = part[k : k + 1, :].astype(jnp.int32)
                j = part[2 + k : 3 + k, :].astype(jnp.int32)
                code = jnp.where(e % 8 == t, (e // 8) * PLANE + j * 8 + b, -1)
                on = (row_ids == code).astype(F32)
                hit.append(on)
            Lf[0:ROWS, b * TOK : (b + 1) * TOK] = hit[0] + hit[1]

        for g in gs:
            gather_far(g)
        pend["wsd"].wait()
        pend["shg"].wait()
        pend["shu"].wait()
        sw = jnp.concatenate([info[b, 6:7, :] for b in range(8)], axis=1)
        sh = jnp.zeros((FS, 8 * TOK), F32)
        for c in range(CHUNKS):
            sh = sh + nt(wsd[:, c * WIDTH : (c + 1) * WIDTH], G[c].reshape(8 * TOK, WIDTH))
        sg, su = swiglu_backward(sh * sw, shg[...].astype(F32), shu[...].astype(F32))
        Lf[ROWS : ROWS + FS, :] = sg
        Lf[ROWS + FS : ROWS + 2 * FS, :] = su
        for b in range(8):
            LT[b] = jnp.transpose(Lf[:, b * TOK : (b + 1) * TOK]).astype(BF)


    for k in range(CHUNKS):
        zin.append(dispatch(k))
        if k >= 1:
            spread(k - 1)
            gather_partner(gs[k - 1])
            forward(gs[k - 1], "near", yh)
            gather_x(gs[k])
        if k == 2:
            pend["wd"].wait()
        if k >= 2:
            spread_on(k - 2)
            forward(gs[k - 2], "partner", yo)
        if k >= 3:
            hidden_all(k - 3)
    gu[:, :, FE:384] = jnp.zeros((4, ROWS, 384 - FE), BF)
    gu[:, :, 384 + FE : DEPTH] = jnp.zeros((4, ROWS, DEPTH - 384 - FE), BF)
    pend["wg"].wait()
    pend["wu"].wait()
    wgu[FE:384, :] = jnp.zeros((384 - FE, D), BF)
    wgu[384 + FE : DEPTH, :] = jnp.zeros((DEPTH - 384 - FE, D), BF)
    pend["sgate"].wait()
    pend["sup"].wait()
    spread(last)
    gather_partner(gs[last])
    forward(gs[last], "near", yh)
    spread_on(last - 1)
    forward(gs[last - 1], "partner", yo)
    hidden_all(last - 2)
    hidden_all(last - 1)
    hidden_of(last, dp)
    act(dp)
    spread_on(last)
    forward(gs[last], "partner", yo)
    pend["wo"].wait()
    gw_ = gather_y(block_of_w)
    gather_x(gw_)
    core_in[last][0].wait_recv()
    hidden_of(last, sib_dp)
    act(sib_dp)
    hidden_of(last, opp_dp)
    act(opp_dp)
    core_in[last][1].wait_recv()
    hidden_of(last, dia_dp)
    act(dia_dp)

    def term(c, d):
        return nn(gu[d], wgu[:, c * WIDTH : (c + 1) * WIDTH])

    def planes(v):
        return v.reshape(8, PLANE, WIDTH).astype(BF)

    t_in, u_in, z_back = [], [], []

    def sum_core(c):
        Ts[c, 0] = planes(term(c, dia_dp))
        a = send(Ts.at[c, 0], Tr.at[c, 0], sib)
        Ts[c, 1] = planes(term(c, sib_dp))
        b = send(Ts.at[c, 1], Tr.at[c, 1], sib)
        t_in.append((a, b))

    def sum_opp(c):
        v = term(c, opp_dp)
        t_in[c][0].wait_recv()
        Us[c] = planes(v + rows_of(Tr[c, 0]))
        u_in.append(send(Us.at[c], Ur.at[c], opp))

    def sum_dp(c):
        v = term(c, dp)
        t_in[c][1].wait_recv()
        v = v + rows_of(Tr[c, 1])
        u_in[c].wait_recv()
        V[c] = planes(v + rows_of(Ur[c]))
        Z[c, z] = V[c, z]
        z_back.append([
            send(V.at[c, (z + dz) % 8], Z.at[c, z], (dp, (z + dz) % 8, t))
            for dz in (1, 7, 2, 6, 3, 5, 4)
        ])

    def partial(c, place):
        w = LT[pl.ds(place * 2, 2)].reshape(2 * TOK, DEPTH)
        return nn(w, Rk[c]).reshape(2, TOK, WIDTH)

    fars, nears, ys = [], [], []

    def sum_far(c):
        for cp in z_back[c]:
            cp.wait_recv()
        Rk[c, 0:ROWS] = rows_of(Z[c]).astype(BF)
        v = partial(c, xf).astype(BF)
        far_s[c, 0] = v[:, 0:HALF]
        far_s[c, 1] = v[:, HALF:TOK]
        fars.append([
            send(far_s.at[c, 0], far_r.at[c, 0], right),
            send(far_s.at[c, 1], far_r.at[c, 1], left),
        ])

    def sum_near(c):
        a = partial(c, xr)
        b = partial(c, xl)
        fars[c][0].wait_recv()
        near_s[c, 0, :, 0:HALF] = (a[:, 0:HALF] + far_r[c, 0].astype(F32)).astype(BF)
        near_s[c, 0, :, HALF:TOK] = a[:, HALF:TOK].astype(BF)
        r = send(near_s.at[c, 0], near_r.at[c, 0], right)
        fars[c][1].wait_recv()
        near_s[c, 1, :, 0:HALF] = b[:, 0:HALF].astype(BF)
        near_s[c, 1, :, HALF:TOK] = (b[:, HALF:TOK] + far_r[c, 1].astype(F32)).astype(BF)
        l = send(near_s.at[c, 1], near_r.at[c, 1], left)
        nears.append((r, l))

    def sum_own(c):
        mine = own.at[c % 2]
        mine[...] = partial(c, x)
        nears[c][0].wait_recv()
        nears[c][1].wait_recv()
        y_s[c] = (
            mine[yo] + near_r[c, 0, yo].astype(F32) + near_r[c, 1, yo].astype(F32)
        ).astype(BF)
        ys.append(send(y_s.at[c], y_r.at[c], across))
        mine[yh] = mine[yh] + near_r[c, 0, yh].astype(F32) + near_r[c, 1, yh].astype(F32)

    def finish(c):
        cols = slice(c * WIDTH, (c + 1) * WIDTH)
        ys[c].wait_recv()
        v = (own[c % 2, yh] + y_r[c].astype(F32) + G[c, t].astype(F32)).astype(BF)
        hid_out[:, cols] = v
        w = nt(v, W[:, :, cols].reshape(D, WIDTH))
        if c == 0:
            ctx[...] = w
        else:
            ctx[...] = ctx[...] + w

    sum_core(0)
    for k in range(CHUNKS + 5):
        if k + 1 < CHUNKS:
            sum_core(k + 1)
        if k == 0:
            gather_partner(gw_)
            forward(gw_, "near", yh)
        if k == 2:
            forward(gw_, "partner", yo)
        if k == CHUNKS:
            gather_far(gw_)
            mine = W.at[:, pl.ds(pl.multiple_of(core * TOK, TOK), TOK)]
            w_in = send(mine, mine, sib)
        if k < CHUNKS:
            sum_opp(k)
        if 0 <= k - 1 < CHUNKS:
            sum_dp(k - 1)
        if k == 1:
            shared_units()
            for cp in ws_in:
                cp.wait()
            for c in range(CHUNKS):
                Rk[c, ROWS + 2 * FS : DEPTH] = jnp.zeros((DEPTH - ROWS - 2 * FS, WIDTH), BF)
        if 0 <= k - 2 < CHUNKS:
            sum_far(k - 2)
        if 0 <= k - 3 < CHUNKS:
            sum_near(k - 3)
        if k == CHUNKS + 1:
            w_in.wait_recv()
        if 0 <= k - 5 < CHUNKS:
            finish(k - 5)
        if 0 <= k - 4 < CHUNKS:
            sum_own(k - 4)
    for b in range(8):
        ctx_s[b] = ctx[:, b * 256 : (b + 1) * 256].astype(BF)
    outs = [
        send(ctx_s.at[p[2]], ctx_r.at[t], p) for p in peers[: len(tens)]
    ]
    ctx_r[t] = ctx_s[t]
    for cp in outs:
        cp.wait_recv()
    ctx_out[...] = ctx_r[...].reshape(8 * TOK, 256)
    for cp in sent:
        cp.wait_send()


def body(
    grad_out, expert_ids, gate_weights, overflow, saved_gate, saved_up, w_gate, w_up, w_down,
    shared_gate_act, shared_up_act, ws_gate, ws_up, ws_down, w_out,
):
    anyspace = pl.BlockSpec(memory_space=pl.ANY)
    vmem = pl.BlockSpec(memory_space=pltpu.VMEM)
    C, W = CHUNKS, WIDTH
    scratch = [
        ((C, 8, TOK, W), BF),
        ((8, 8, TOK), F32),
        ((C, 8, PLANE, W), BF),
        ((C, 4, 8, PLANE, W), BF),
        ((C, 2, 8, PLANE, W), BF),
        ((C, 2, 8, PLANE, W), BF),
        ((C, 8, PLANE, W), BF),
        ((C, 8, PLANE, W), BF),
        ((C, 8, PLANE, W), BF),
        ((C, 8, PLANE, W), BF),
        ((C, 2, 2, TOK // 2, W), BF),
        ((C, 2, 2, TOK, W), BF),
        ((C, TOK, W), BF),
        ((C, 2, 2, TOK // 2, W), BF),
        ((C, 2, 2, TOK, W), BF),
        ((C, TOK, W), BF),
        ((8, 256, D), BF),
        ((FE, D), BF),
        ((DEPTH, D), BF),
        ((FS, D), BF),
        ((4, CAP, 64, FE), BF),
        ((4, CAP, 64, FE), BF),
        ((FS, 8 * TOK), BF),
        ((FS, 8 * TOK), BF),
        ((4, ROWS, FE), F32),
        ((4, ROWS, DEPTH), BF),
        ((C, 8, PLANE, W), BF),
        ((C, 8, PLANE, W), BF),
        ((ROWS, ROWS), BF),
        ((DEPTH, 8 * TOK), F32),
        ((8, TOK, DEPTH), BF),
        ((C, DEPTH, W), BF),
        ((2, 2, TOK, W), F32),
        ((TOK, D), F32),
        ((8, TOK, 256), BF),
        ((8, TOK, 256), BF),
    ]
    return pl.pallas_call(
        kernel,
        out_shape=(
            jax.ShapeDtypeStruct((TOK, D), BF),
            jax.ShapeDtypeStruct((8 * TOK, 256), BF),
        ),
        in_specs=[anyspace, vmem, vmem, vmem] + [anyspace] * 11,
        out_specs=(vmem, vmem),
        scratch_shapes=[pltpu.VMEM(s, d) for s, d in scratch]
        + [pltpu.SemaphoreType.DMA((N_SEM,))] * 2
        + [pltpu.SemaphoreType.DMA((32,))],
        compiler_params=pltpu.CompilerParams(
            collective_id=0, has_side_effects=True, vmem_limit_bytes=63 * 1024 * 1024
        ),
        name="layer",
    )(
        grad_out,
        expert_ids.T,
        gate_weights.T,
        overflow.T,
        saved_gate[0].transpose(0, 2, 1, 3),
        saved_up[0].transpose(0, 2, 1, 3),
        w_gate[0].T,
        w_up[0].T,
        w_down[0],
        shared_gate_act.T,
        shared_up_act.T,
        ws_gate.T,
        ws_up.T,
        ws_down,
        w_out,
    )


def solution(mesh):
    in_specs = (
        P(("dp", "expert", "tensor"), None),
        P(("dp", "expert", "tensor"), None),
        P(("dp", "expert", "tensor"), None),
        P(("dp", "expert", "tensor"), None),
        P(("expert", "tensor"), None, None, None, "dp"),
        P(("expert", "tensor"), None, None, None, "dp"),
        P(("expert", "tensor"), None, "dp"),
        P(("expert", "tensor"), None, "dp"),
        P(("expert", "tensor"), "dp", None),
        P(("dp", "expert"), "tensor"),
        P(("dp", "expert"), "tensor"),
        P(None, "tensor"),
        P(None, "tensor"),
        P("tensor", None),
        P("tensor", None),
    )
    out_specs = (P(("dp", "expert", "tensor"), None), P(("dp", "expert"), "tensor"))
    return jax.shard_map(body, mesh=mesh, in_specs=in_specs, out_specs=out_specs, check_vma=False)
```

```python
import functools

import jax
import jax.numpy as jnp
from jax import lax
from jax.experimental import pallas as pl
from jax.experimental.pallas import tpu as pltpu
from jax.sharding import PartitionSpec as P

MESH = pl.DeviceIdType.MESH
BF = jnp.bfloat16
F32 = jnp.float32
CHUNKS = 4
TOK = 128
D = 2048
WIDTH = D // CHUNKS
CAP = 5
PLANE = CAP * 8
ROWS = 8 * PLANE
FE = 352
FS = 176
DEPTH = 768
N_SEM = 260
HALF = TOK // 2


def nn(a, b):
    return jnp.dot(a, b, preferred_element_type=F32)


def nt(a, b):
    return lax.dot_general(a, b, (((1,), (1,)), ((), ())), preferred_element_type=F32)


def swiglu_backward(hidden, gate_act, up_act):
    s = jax.nn.sigmoid(gate_act)
    gate = hidden * up_act * s * (1.0 + gate_act * (1.0 - s))
    up = hidden * gate_act * s
    return gate, up


def rows_of(planes):
    return planes.astype(F32).reshape(ROWS, planes.shape[-1])


def kernel(
    grad_ref, ids_ref, gw_ref, ov_ref, sgate_hbm, sup_hbm, wg_hbm, wu_hbm, wd_hbm,
    shg_hbm, shu_hbm, wsg_hbm, wsu_hbm, wsd_hbm, wo_hbm,
    hid_out, ctx_out,
    G, info, zs, A, Ts, Tr, Us, Ur, V, Z, far_s, near_s, y_s, far_r, near_r, y_r, W,
    wd, wgu, wsd, sgate, sup, shg, shu, hid, gu, Xs, Xr, Q, Lf, LT, Rk, own, ctx, ctx_s, ctx_r,
    ss, rs, ls,
):
    dp, z, t = lax.axis_index("dp"), lax.axis_index("expert"), lax.axis_index("tensor")
    ylo, core, x, yh = dp // 2, dp % 2, t // 2, t % 2
    xr, xl, xf = (x + 1) % 4, (x + 3) % 4, (x + 2) % 4
    yo = 1 - yh
    right, left, across = (dp, z, xr * 2 + yh), (dp, z, xl * 2 + yh), (dp, z, x * 2 + yo)
    sib = (ylo * 2 + 1 - core, z, t)
    opp = ((1 - ylo) * 2 + core, z, t)
    sib_dp, opp_dp, dia_dp = ylo * 2 + 1 - core, (1 - ylo) * 2 + core, (1 - ylo) * 2 + 1 - core

    count = [0]
    sent = []

    def send(src, dst, dev):
        i = count[0]
        count[0] += 1
        cp = pltpu.make_async_remote_copy(
            src_ref=src, dst_ref=dst, send_sem=ss.at[i], recv_sem=rs.at[i],
            device_id=dev, device_id_type=MESH,
        )
        cp.start()
        sent.append(cp)
        return cp

    locals_ = [0]

    def fetch(src, dst):
        i = locals_[0]
        locals_[0] += 1
        cp = pltpu.make_async_copy(src, dst, ls.at[i])
        cp.start()
        return cp

    tens = [(dx, dy) for dx in range(4) for dy in range(2) if dx or dy]

    own_in = [fetch(grad_ref.at[:, pl.ds(c * WIDTH, WIDTH)], G.at[c, t]) for c in range(CHUNKS)]
    barrier = pltpu.get_barrier_semaphore()
    peers = [(dp, z, ((x + dx) % 4) * 2 + (yh + dy) % 2) for dx, dy in tens]
    peers += [(dp, (z + dz) % 8, t) for dz in range(1, 8)]
    peers += [sib, opp]
    for p in peers:
        pl.semaphore_signal(barrier, inc=1, device_id=p, device_id_type=MESH)

    pend = dict(
        wd=fetch(wd_hbm, wd),
        wsd=fetch(wsd_hbm, wsd),
        wg=fetch(wg_hbm, wgu.at[pl.ds(0, FE)]),
        wu=fetch(wu_hbm, wgu.at[pl.ds(384, FE)]),
        wo=fetch(
            wo_hbm.at[pl.ds(pl.multiple_of(core * TOK, TOK), TOK)],
            W.at[t, pl.ds(pl.multiple_of(core * TOK, TOK), TOK)],
        ),
        sgate=fetch(sgate_hbm, sgate),
        sup=fetch(sup_hbm, sup),
        shg=fetch(shg_hbm, shg),
        shu=fetch(shu_hbm, shu),
    )
    ws_in = []
    for c in range(CHUNKS):
        cols = pl.ds(c * WIDTH, WIDTH)
        ws_in.append(fetch(wsg_hbm.at[:, cols], Rk.at[c, pl.ds(ROWS, FS)]))
        ws_in.append(fetch(wsu_hbm.at[:, cols], Rk.at[c, pl.ds(ROWS + FS, FS)]))

    ids = ids_ref[...]
    gw = gw_ref[...]
    ov = ov_ref[...].astype(F32)
    experts = lax.broadcasted_iota(jnp.int32, (64, TOK), 0)
    oh = [(experts == ids[k : k + 1, :]).astype(F32) for k in range(2)]
    upper = lax.broadcasted_iota(jnp.int32, (TOK, TOK), 0) < lax.broadcasted_iota(
        jnp.int32, (TOK, TOK), 1
    )
    earlier = nn((oh[0] + oh[1]).astype(BF), upper.astype(F32).astype(BF))
    slots = [jnp.sum(earlier * oh[k], axis=0, keepdims=True) for k in range(2)]
    routed_weight = (gw * (1.0 - ov)).astype(BF).astype(F32)
    shared_weight = 1.0 + jnp.sum(gw * ov, axis=0, keepdims=True)
    info[t] = jnp.concatenate(
        [ids.astype(F32), slots[0], slots[1], routed_weight, shared_weight, shared_weight], axis=0
    )

    row_ids = lax.broadcasted_iota(jnp.int32, (ROWS, TOK), 0)
    weight = jnp.zeros((ROWS, 1), F32)
    pick = jnp.zeros((ROWS, TOK), F32)
    for k in range(2):
        e = ids[k : k + 1, :]
        code = (e % 8) * PLANE + (e // 8) * CAP + slots[k].astype(jnp.int32)
        on = (row_ids == code).astype(F32)
        weight = weight + jnp.sum(on * routed_weight[k : k + 1, :], axis=1, keepdims=True)
        pick = pick + on
    pick = pick.astype(BF)
    r = lax.broadcasted_iota(jnp.int32, (ROWS, ROWS), 0)
    from_row = (r % 8) * PLANE + (r // PLANE) * CAP + (r % PLANE) // 8
    Q[...] = (lax.broadcasted_iota(jnp.int32, (ROWS, ROWS), 1) == from_row).astype(F32).astype(BF)

    def pick_rows(c):
        own_in[c].wait()
        Xs[c] = (nn(pick, G[c, t]) * weight).reshape(8, PLANE, WIDTH).astype(BF)
        Xr[c, t] = Xs[c, t]

    pick_rows(0)
    pl.semaphore_wait(barrier, len(peers))

    def block_of_tokens(c):
        def view(i, part=None):
            return G.at[c, i] if part is None else G.at[c, i, pl.ds(part * HALF, HALF)]

        return view

    def block_of_w(i, part=None):
        if part is None:
            return W.at[i, pl.ds(pl.multiple_of(core * TOK, TOK), TOK)]
        return W.at[i, pl.ds(pl.multiple_of(core * TOK + part * HALF, HALF), HALF)]

    def gather_y(view):
        return dict(view=view, y=send(view(t), view(t), across), far=[])

    def gather_x(g):
        src = g["view"](t)
        g["near"] = [send(src, src, right), send(src, src, left)]

    def gather_partner(g):
        g["y"].wait_recv()
        src = g["view"](x * 2 + yo)
        g["partner"] = [send(src, src, right), send(src, src, left)]

    def forward(g, kind, half):
        for cp in g[kind]:
            cp.wait_recv()
        a = g["view"](xl * 2 + half, 0)
        b = g["view"](xr * 2 + half, 1)
        g["far"] += [send(a, a, right), send(b, b, left)]

    def gather_far(g):
        for cp in g["far"]:
            cp.wait_recv()

    x_in = []
    for c in range(CHUNKS):
        if c:
            pick_rows(c)
        x_in.append([send(Xs.at[c, p[2]], Xr.at[c, t], p) for p in peers[: len(tens)]])
        if c == 1:
            infos = [send(info.at[t], info.at[t], p) for p in peers[: len(tens)]]
    gs = [gather_y(block_of_tokens(c)) for c in range(CHUNKS)]
    gather_x(gs[0])

    def dispatch(c):
        for cp in x_in[c]:
            cp.wait_recv()
        zs[c] = nn(Q[...], rows_of(Xr[c]).astype(BF)).reshape(8, PLANE, WIDTH).astype(BF)
        A[c, dp, z] = zs[c, z]
        return [
            send(zs.at[c, (z + dz) % 8], A.at[c, dp, z], (dp, (z + dz) % 8, t))
            for dz in (1, 7, 2, 6, 3, 5, 4)
        ]

    zin, core_in, opp_in = [], [], []
    last = CHUNKS - 1

    def spread(c):
        for cp in zin[c]:
            cp.wait_recv()
        opp_in.append(send(A.at[c, dp], A.at[c, dp], opp))
        core_in.append([send(A.at[c, dp], A.at[c, dp], sib)])

    def spread_on(c):
        opp_in[c].wait_recv()
        core_in[c].append(send(A.at[c, opp_dp], A.at[c, opp_dp], sib))

    def hidden_of(c, d):
        w = wd[:, c * WIDTH : (c + 1) * WIDTH]
        h = nt(rows_of(A[c, d]).astype(BF), w)
        if c == 0:
            hid[d] = h
        else:
            hid[d] = hid[d] + h

    def hidden_all(c):
        hidden_of(c, dp)
        hidden_of(c, opp_dp)
        for cp in core_in[c]:
            cp.wait_recv()
        hidden_of(c, sib_dp)
        hidden_of(c, dia_dp)

    def act(d):
        h4 = hid[d].reshape(8, CAP, 8, FE)
        gs, us = [], []
        for j in range(CAP):
            g, u = swiglu_backward(
                h4[:, j],
                sgate[d, j].astype(F32).reshape(8, 8, FE),
                sup[d, j].astype(F32).reshape(8, 8, FE),
            )
            gs.append(g)
            us.append(u)
        gu[d, :, 0:FE] = jnp.stack(gs, axis=1).reshape(ROWS, FE).astype(BF)
        gu[d, :, 384 : 384 + FE] = jnp.stack(us, axis=1).reshape(ROWS, FE).astype(BF)

    def shared_units():
        for cp in infos:
            cp.wait_recv()
        row_ids = lax.broadcasted_iota(jnp.int32, (ROWS, TOK), 0)
        Lf[ROWS + 2 * FS : DEPTH, :] = jnp.zeros((DEPTH - ROWS - 2 * FS, 8 * TOK), F32)
        for b in range(8):
            part = info[b]
            hit = []
            for k in range(2):
                e = part[k : k + 1, :].astype(jnp.int32)
                j = part[2 + k : 3 + k, :].astype(jnp.int32)
                code = jnp.where(e % 8 == t, (e // 8) * PLANE + j * 8 + b, -1)
                on = (row_ids == code).astype(F32)
                hit.append(on)
            Lf[0:ROWS, b * TOK : (b + 1) * TOK] = hit[0] + hit[1]

        for g in gs:
            gather_far(g)
        pend["wsd"].wait()
        pend["shg"].wait()
        pend["shu"].wait()
        sw = jnp.concatenate([info[b, 6:7, :] for b in range(8)], axis=1)
        sh = jnp.zeros((FS, 8 * TOK), F32)
        for c in range(CHUNKS):
            sh = sh + nt(wsd[:, c * WIDTH : (c + 1) * WIDTH], G[c].reshape(8 * TOK, WIDTH))
        sg, su = swiglu_backward(sh * sw, shg[...].astype(F32), shu[...].astype(F32))
        Lf[ROWS : ROWS + FS, :] = sg
        Lf[ROWS + FS : ROWS + 2 * FS, :] = su
        for b in range(8):
            LT[b] = jnp.transpose(Lf[:, b * TOK : (b + 1) * TOK]).astype(BF)


    for k in range(CHUNKS):
        zin.append(dispatch(k))
        if k >= 1:
            spread(k - 1)
            gather_partner(gs[k - 1])
            forward(gs[k - 1], "near", yh)
            gather_x(gs[k])
        if k == 2:
            pend["wd"].wait()
        if k >= 2:
            spread_on(k - 2)
            forward(gs[k - 2], "partner", yo)
        if k >= 3:
            hidden_all(k - 3)
    gu[:, :, FE:384] = jnp.zeros((4, ROWS, 384 - FE), BF)
    gu[:, :, 384 + FE : DEPTH] = jnp.zeros((4, ROWS, DEPTH - 384 - FE), BF)
    pend["wg"].wait()
    pend["wu"].wait()
    wgu[FE:384, :] = jnp.zeros((384 - FE, D), BF)
    wgu[384 + FE : DEPTH, :] = jnp.zeros((DEPTH - 384 - FE, D), BF)
    pend["sgate"].wait()
    pend["sup"].wait()
    spread(last)
    gather_partner(gs[last])
    forward(gs[last], "near", yh)
    pend["wo"].wait()
    gw_ = dict(view=block_of_w, far=[])
    gather_x(gw_)
    spread_on(last - 1)
    forward(gs[last - 1], "partner", yo)
    hidden_all(last - 2)
    hidden_all(last - 1)
    hidden_of(last, dp)
    act(dp)
    spread_on(last)
    forward(gs[last], "partner", yo)
    gw_["y"] = gather_y(block_of_w)["y"]
    core_in[last][0].wait_recv()
    hidden_of(last, sib_dp)
    act(sib_dp)
    hidden_of(last, opp_dp)
    act(opp_dp)
    core_in[last][1].wait_recv()
    hidden_of(last, dia_dp)
    act(dia_dp)

    def term(c, d):
        return nn(gu[d], wgu[:, c * WIDTH : (c + 1) * WIDTH])

    def planes(v):
        return v.reshape(8, PLANE, WIDTH).astype(BF)

    t_in, u_in, z_back = [], [], []

    def sum_core(c):
        Ts[c, 0] = planes(term(c, dia_dp))
        a = send(Ts.at[c, 0], Tr.at[c, 0], sib)
        Ts[c, 1] = planes(term(c, sib_dp))
        b = send(Ts.at[c, 1], Tr.at[c, 1], sib)
        t_in.append((a, b))

    def sum_opp(c):
        v = term(c, opp_dp)
        t_in[c][0].wait_recv()
        Us[c] = planes(v + rows_of(Tr[c, 0]))
        u_in.append(send(Us.at[c], Ur.at[c], opp))

    def sum_dp(c):
        v = term(c, dp)
        t_in[c][1].wait_recv()
        v = v + rows_of(Tr[c, 1])
        u_in[c].wait_recv()
        V[c] = planes(v + rows_of(Ur[c]))
        Z[c, z] = V[c, z]
        z_back.append([
            send(V.at[c, (z + dz) % 8], Z.at[c, z], (dp, (z + dz) % 8, t))
            for dz in (1, 7, 2, 6, 3, 5, 4)
        ])

    def partial(c, place):
        w = LT[pl.ds(place * 2, 2)].reshape(2 * TOK, DEPTH)
        return nn(w, Rk[c]).reshape(2, TOK, WIDTH)

    fars, nears, ys = [], [], []

    def sum_far(c):
        for cp in z_back[c]:
            cp.wait_recv()
        Rk[c, 0:ROWS] = rows_of(Z[c]).astype(BF)
        v = partial(c, xf).astype(BF)
        far_s[c, 0] = v[:, 0:HALF]
        far_s[c, 1] = v[:, HALF:TOK]
        fars.append([
            send(far_s.at[c, 0], far_r.at[c, 0], right),
            send(far_s.at[c, 1], far_r.at[c, 1], left),
        ])

    def sum_near(c):
        a = partial(c, xr)
        b = partial(c, xl)
        fars[c][0].wait_recv()
        near_s[c, 0, :, 0:HALF] = (a[:, 0:HALF] + far_r[c, 0].astype(F32)).astype(BF)
        near_s[c, 0, :, HALF:TOK] = a[:, HALF:TOK].astype(BF)
        r = send(near_s.at[c, 0], near_r.at[c, 0], right)
        fars[c][1].wait_recv()
        near_s[c, 1, :, 0:HALF] = b[:, 0:HALF].astype(BF)
        near_s[c, 1, :, HALF:TOK] = (b[:, HALF:TOK] + far_r[c, 1].astype(F32)).astype(BF)
        l = send(near_s.at[c, 1], near_r.at[c, 1], left)
        nears.append((r, l))

    def sum_own(c):
        mine = own.at[c % 2]
        mine[...] = partial(c, x)
        nears[c][0].wait_recv()
        nears[c][1].wait_recv()
        y_s[c] = (
            mine[yo] + near_r[c, 0, yo].astype(F32) + near_r[c, 1, yo].astype(F32)
        ).astype(BF)
        ys.append(send(y_s.at[c], y_r.at[c], across))
        mine[yh] = mine[yh] + near_r[c, 0, yh].astype(F32) + near_r[c, 1, yh].astype(F32)

    def finish(c):
        cols = slice(c * WIDTH, (c + 1) * WIDTH)
        ys[c].wait_recv()
        v = (own[c % 2, yh] + y_r[c].astype(F32) + G[c, t].astype(F32)).astype(BF)
        hid_out[:, cols] = v

    def project(c):
        cols = slice(c * WIDTH, (c + 1) * WIDTH)
        w = nt(hid_out[:, cols], W[:, :, cols].reshape(D, WIDTH))
        if c == 0:
            ctx[...] = w
        else:
            ctx[...] = ctx[...] + w

    sum_core(0)
    for k in range(CHUNKS + 5):
        if k + 1 < CHUNKS:
            sum_core(k + 1)
        if k < CHUNKS:
            sum_opp(k)
        if k == 0:
            gather_partner(gw_)
            forward(gw_, "near", yh)
        if k == 2:
            forward(gw_, "partner", yo)
        if 0 <= k - 1 < CHUNKS:
            sum_dp(k - 1)
        if k == 2:
            shared_units()
            for cp in ws_in:
                cp.wait()
            for c in range(CHUNKS):
                Rk[c, ROWS + 2 * FS : DEPTH] = jnp.zeros((DEPTH - ROWS - 2 * FS, WIDTH), BF)
        if 0 <= k - 2 < CHUNKS:
            sum_far(k - 2)
        if 0 <= k - 3 < CHUNKS:
            sum_near(k - 3)
        if k == CHUNKS:
            gather_far(gw_)
            mine = W.at[:, pl.ds(pl.multiple_of(core * TOK, TOK), TOK)]
            w_in = send(mine, mine, sib)
        if 0 <= k - 5 < CHUNKS:
            finish(k - 5)
        if 0 <= k - 4 < CHUNKS:
            sum_own(k - 4)
        if k == CHUNKS + 2:
            w_in.wait_recv()
        if 0 <= k - 6 < CHUNKS:
            project(k - 6)
    for c in range(CHUNKS - 1, CHUNKS):
        project(c)
    for b in range(8):
        ctx_s[b] = ctx[:, b * 256 : (b + 1) * 256].astype(BF)
    outs = [
        send(ctx_s.at[p[2]], ctx_r.at[t], p) for p in peers[: len(tens)]
    ]
    ctx_r[t] = ctx_s[t]
    for cp in outs:
        cp.wait_recv()
    ctx_out[...] = ctx_r[...].reshape(8 * TOK, 256)
    for cp in sent:
        cp.wait_send()


def body(
    grad_out, expert_ids, gate_weights, overflow, saved_gate, saved_up, w_gate, w_up, w_down,
    shared_gate_act, shared_up_act, ws_gate, ws_up, ws_down, w_out,
):
    anyspace = pl.BlockSpec(memory_space=pl.ANY)
    vmem = pl.BlockSpec(memory_space=pltpu.VMEM)
    C, W = CHUNKS, WIDTH
    scratch = [
        ((C, 8, TOK, W), BF),
        ((8, 8, TOK), F32),
        ((C, 8, PLANE, W), BF),
        ((C, 4, 8, PLANE, W), BF),
        ((C, 2, 8, PLANE, W), BF),
        ((C, 2, 8, PLANE, W), BF),
        ((C, 8, PLANE, W), BF),
        ((C, 8, PLANE, W), BF),
        ((C, 8, PLANE, W), BF),
        ((C, 8, PLANE, W), BF),
        ((C, 2, 2, TOK // 2, W), BF),
        ((C, 2, 2, TOK, W), BF),
        ((C, TOK, W), BF),
        ((C, 2, 2, TOK // 2, W), BF),
        ((C, 2, 2, TOK, W), BF),
        ((C, TOK, W), BF),
        ((8, 256, D), BF),
        ((FE, D), BF),
        ((DEPTH, D), BF),
        ((FS, D), BF),
        ((4, CAP, 64, FE), BF),
        ((4, CAP, 64, FE), BF),
        ((FS, 8 * TOK), BF),
        ((FS, 8 * TOK), BF),
        ((4, ROWS, FE), F32),
        ((4, ROWS, DEPTH), BF),
        ((C, 8, PLANE, W), BF),
        ((C, 8, PLANE, W), BF),
        ((ROWS, ROWS), BF),
        ((DEPTH, 8 * TOK), F32),
        ((8, TOK, DEPTH), BF),
        ((C, DEPTH, W), BF),
        ((2, 2, TOK, W), F32),
        ((TOK, D), F32),
        ((8, TOK, 256), BF),
        ((8, TOK, 256), BF),
    ]
    shapes = (
        jax.ShapeDtypeStruct((TOK, D), BF),
        jax.ShapeDtypeStruct((8 * TOK, 256), BF),
    )
    made = pl.pallas_call(
        kernel,
        out_shape=shapes,
        in_specs=[anyspace, vmem, vmem, vmem] + [anyspace] * 11,
        out_specs=(vmem, vmem),
        scratch_shapes=[pltpu.VMEM(s, d) for s, d in scratch]
        + [pltpu.SemaphoreType.DMA((N_SEM,))] * 2
        + [pltpu.SemaphoreType.DMA((32,))],
        compiler_params=pltpu.CompilerParams(
            collective_id=0, has_side_effects=True, vmem_limit_bytes=63 * 1024 * 1024
        ),
        name="layer",
    )(
        grad_out,
        expert_ids.T,
        gate_weights.T,
        overflow.T,
        saved_gate[0].transpose(0, 2, 1, 3),
        saved_up[0].transpose(0, 2, 1, 3),
        w_gate[0].T,
        w_up[0].T,
        w_down[0],
        shared_gate_act.T,
        shared_up_act.T,
        ws_gate.T,
        ws_up.T,
        ws_down,
        w_out,
    )
    return made


def solution(mesh):
    in_specs = (
        P(("dp", "expert", "tensor"), None),
        P(("dp", "expert", "tensor"), None),
        P(("dp", "expert", "tensor"), None),
        P(("dp", "expert", "tensor"), None),
        P(("expert", "tensor"), None, None, None, "dp"),
        P(("expert", "tensor"), None, None, None, "dp"),
        P(("expert", "tensor"), None, "dp"),
        P(("expert", "tensor"), None, "dp"),
        P(("expert", "tensor"), "dp", None),
        P(("dp", "expert"), "tensor"),
        P(("dp", "expert"), "tensor"),
        P(None, "tensor"),
        P(None, "tensor"),
        P("tensor", None),
        P("tensor", None),
    )
    out_specs = (P(("dp", "expert", "tensor"), None), P(("dp", "expert"), "tensor"))
    return jax.shard_map(body, mesh=mesh, in_specs=in_specs, out_specs=out_specs, check_vma=False)
```
